256 devices in a mesh: tm: 4 (over y_lo, core), space: 64 (over x, y_hi, z).
Axes of the slice: x: 4, y: 4 (y_hi: 2, y_lo: 2; y = y_hi * 2 + y_lo), z: 8, core: 2. Of those that a mesh axis runs over, the one named last changes fastest.
Arguments:
- query_in: bfloat16 [16, 64, 2, 20, 2560], P('tm', 'space'), may hold values from -120 to 120
- key_in: bfloat16 [16, 64, 2, 20, 2560], P('tm', 'space'), may hold values from -120 to 120
- value_in: bfloat16 [16, 64, 2, 20, 2560], P('tm', 'space'), may hold values from -6 to 6
- out_grad: bfloat16 [16, 64, 2, 20, 2560], P('tm', 'space'), may hold values from -6 to 6
- norm_gains: float32 [2, 2560], replicated, may hold values from 0.25 to 1.75
Outputs:
- attn_out: bfloat16 [16, 64, 2, 20, 2560], P('tm', 'space')
- query_grad: bfloat16 [16, 64, 2, 20, 2560], P('tm', 'space')
- key_grad: bfloat16 [16, 64, 2, 20, 2560], P('tm', 'space')
- value_grad: bfloat16 [16, 64, 2, 20, 2560], P('tm', 'space')
- gain_grads: float32 [2, 2560], P(None, 'space')
The draws below stay inside these ranges and needn't reach their ends.
All inputs are finite; a program needn't handle non-finite values.
Results may differ from the reference program's by a relative error of at most 0.04.
Values may be sent and summed in bfloat16 or wider, within the bound.
A program may use at most 64 MiB of HBM per device.

```python
import jax
import jax.numpy as jnp
from jax import lax

HEADS = 20
HDIM = 128
TILE_COLS = 20
TILE_ROWS = 2
HD = 2560
FRAMES = 16
TILES = 64
ROWS = 32
COLS = 80


def tile_layout(values):
    arranged = values.reshape(FRAMES, ROWS // TILE_ROWS, TILE_ROWS, 4, TILE_COLS, HD).transpose(0, 1, 3, 2, 4, 5)
    return arranged.reshape(FRAMES, TILES, TILE_ROWS, TILE_COLS, HD)


def shared_parts(key):
    subkeys = jax.random.split(key, 1)
    tiles = ROWS // TILE_ROWS * (COLS // TILE_COLS)
    pairing = jax.random.permutation(subkeys[0], tiles)
    return pairing


def scaled_field(key, jitter, pairing):
    subkeys = jax.random.split(key, 2)
    row_scale = jnp.exp(jax.random.uniform(subkeys[0], (FRAMES, ROWS, COLS, 1)) * 2.3)
    feature_scale = jnp.exp(jax.random.uniform(subkeys[1], (HD,)) * 2.3)
    tiles = ROWS // TILE_ROWS * (COLS // TILE_COLS)
    tile = (jnp.arange(ROWS) // TILE_ROWS)[:, None] * (COLS // TILE_COLS) + (jnp.arange(COLS) // TILE_COLS)[None, :]
    feature_block = jnp.arange(HD) // (HD // tiles)
    boosted = jnp.where(pairing[tile][:, :, None] == feature_block[None, None, :], 3.0, 1.0)
    return jitter * row_scale * feature_scale * boosted * 0.1


def draw_query_in(key, part):
    pairing = shared_parts(key)
    key = jax.random.fold_in(key, 11)
    subkeys = jax.random.split(key, 2)
    full_shape = (FRAMES, ROWS, COLS, HD)
    jitter = jnp.clip(jax.random.normal(subkeys[0], full_shape), -4.0, 4.0)
    values_out = scaled_field(subkeys[1], jitter, pairing)
    return tile_layout(values_out).astype(jnp.bfloat16)


def draw_key_in(key, part):
    pairing = shared_parts(key)
    key = jax.random.fold_in(key, 23)
    subkeys = jax.random.split(key, 2)
    full_shape = (FRAMES, ROWS, COLS, HD)
    jitter = jnp.clip(jax.random.normal(subkeys[0], full_shape), -4.0, 4.0)
    values_out = scaled_field(subkeys[1], jitter, pairing)
    return tile_layout(values_out).astype(jnp.bfloat16)


def steps_of(key, dims, cuts, least, largest):
    gain = 1.0
    for position, shards_of in cuts:
        draws = jax.random.uniform(jax.random.fold_in(jax.random.fold_in(key, 6), position), (shards_of,), jnp.float32, least / len(cuts), largest / len(cuts))
        gain = gain * jnp.repeat(jnp.exp(draws), dims[position] // shards_of).reshape((-1,) + (1,) * (len(dims) - 1 - position))
    return gain


def noise(stream_key, extent, width, reach, pieces=(), kind=jnp.bfloat16):
    drawn = jax.random.normal(stream_key, extent, jnp.float32) * width
    if len(pieces) > 0:
        drawn = steps_of(stream_key, extent, pieces, -0.22, 0.18) * drawn
    return jnp.clip(drawn, min=-reach, max=reach).astype(kind)


def setup_inputs(seed: int = 0) -> dict:
    arg_keys = jax.random.split(jax.random.key(seed), 6)
    query_in = draw_query_in(jax.random.fold_in(arg_keys[5], 71), 0)
    key_in = draw_key_in(jax.random.fold_in(arg_keys[5], 71), 0)
    value_in = noise(arg_keys[2], (FRAMES, TILES, TILE_ROWS, TILE_COLS, HD), 1.0, 6.0, ((0, 4), (1, 64)))
    out_grad = noise(arg_keys[3], (FRAMES, TILES, TILE_ROWS, TILE_COLS, HD), 1.0, 6.0, ((0, 4), (1, 64)))
    norm_gains = jnp.clip(1.0 + 0.15 * jax.random.normal(arg_keys[4], (2, HD), jnp.float32), 0.25, 1.75)
    return {"query_in": query_in, "key_in": key_in, "value_in": value_in, "out_grad": out_grad, "norm_gains": norm_gains}


EPSILON = 1e-06
GRID_COLS = 4

def rounded(values):
    return lax.optimization_barrier(values.astype(jnp.bfloat16)).astype(jnp.float32)

def rms_scale(values):
    return lax.rsqrt(lax.optimization_barrier(jnp.mean(values * values, axis=-1, keepdims=True)) + EPSILON)

def to_grid(values):
    frame_count, tile_count, tile_rows, tile_cols, features = values.shape
    grid_rows = tile_count // GRID_COLS
    arranged = values.reshape(frame_count, grid_rows, GRID_COLS, tile_rows, tile_cols, features).transpose(0, 1, 3, 2, 4, 5)
    return arranged.reshape(frame_count, grid_rows * tile_rows, GRID_COLS * tile_cols, features)

def to_tiles(values):
    frame_count, row_count, column_count, features = values.shape
    grid_rows = row_count // TILE_ROWS
    arranged = values.reshape(frame_count, grid_rows, TILE_ROWS, GRID_COLS, TILE_COLS, features).transpose(0, 1, 3, 2, 4, 5)
    return arranged.reshape(frame_count, grid_rows * GRID_COLS, TILE_ROWS, TILE_COLS, features)

def window_ids(frames, rows, cols):
    return ((frames + 2) // 4, (rows + TILE_ROWS // 2) // TILE_ROWS, (cols + TILE_COLS // 2) // TILE_COLS)

def window_attention(operands):
    normed_q, normed_k, values, cotangent, usable = operands
    token_count, features = normed_q.shape
    inverse_root = HDIM ** (-0.5)
    query_heads = normed_q.astype(jnp.float32).reshape(token_count, HEADS, HDIM)
    key_heads = normed_k.astype(jnp.float32).reshape(token_count, HEADS, HDIM)
    value_heads = values.astype(jnp.float32).reshape(token_count, HEADS, HDIM)
    grad_heads = cotangent.astype(jnp.float32).reshape(token_count, HEADS, HDIM)
    scores = jnp.einsum('qhd,khd->hqk', query_heads, key_heads) * inverse_root
    scores = jnp.where(usable[None, :, :], scores, -1e+30)
    highest = lax.optimization_barrier(jnp.max(scores, axis=-1, keepdims=True))
    weights = jnp.exp(scores - highest)
    probs_full = weights / lax.optimization_barrier(jnp.sum(weights, axis=-1, keepdims=True))
    probs = rounded(probs_full)
    attended = jnp.einsum('hqk,khd->qhd', probs, value_heads).astype(jnp.bfloat16)
    row_terms = lax.optimization_barrier(jnp.sum(grad_heads * lax.optimization_barrier(attended).astype(jnp.float32), axis=-1))
    products = jnp.einsum('qhd,khd->hqk', grad_heads, value_heads)
    score_grads = rounded(probs_full * (products - jnp.transpose(row_terms)[:, :, None]) * inverse_root)
    grad_query = jnp.einsum('hqk,khd->qhd', score_grads, key_heads).reshape(token_count, features)
    grad_key = jnp.einsum('hqk,qhd->khd', score_grads, query_heads).reshape(token_count, features)
    grad_value = jnp.einsum('hqk,qhd->khd', probs, grad_heads).reshape(token_count, features)
    return jnp.stack([attended.reshape(token_count, features), grad_query.astype(jnp.bfloat16), grad_key.astype(jnp.bfloat16), grad_value.astype(jnp.bfloat16)])

def reference(query_in, key_in, value_in, out_grad, norm_gains):
    query_in = to_grid(query_in)
    key_in = to_grid(key_in)
    value_in = to_grid(value_in)
    out_grad = to_grid(out_grad)
    frame_count, row_count, column_count, features = query_in.shape
    grid_rows = row_count // TILE_ROWS
    time_blocks = frame_count // 4
    window_tokens = 4 * TILE_ROWS * TILE_COLS
    query_full = query_in.astype(jnp.float32)
    key_full = key_in.astype(jnp.float32)
    query_scale = rms_scale(query_full)
    key_scale = rms_scale(key_full)
    normed_query = (query_full * query_scale * norm_gains[0]).astype(jnp.bfloat16)
    normed_key = (key_full * key_scale * norm_gains[1]).astype(jnp.bfloat16)
    shifts = (-2, -(TILE_ROWS // 2), -(TILE_COLS // 2))
    moved = jnp.roll(jnp.stack([normed_query, normed_key, value_in, out_grad]), shifts, axis=(1, 2, 3))
    zero = jnp.zeros((), jnp.int32)

    def arrange(ids):
        full = jnp.broadcast_to(ids, (4, TILE_ROWS, column_count))
        return full.reshape(4, TILE_ROWS, GRID_COLS, TILE_COLS).transpose(2, 0, 1, 3).reshape(GRID_COLS, window_tokens)

    def block(index):
        time_block = index // grid_rows
        row_block = index % grid_rows
        piece = lax.dynamic_slice(moved, (zero, time_block * 4, row_block * TILE_ROWS, zero, zero), (4, 4, TILE_ROWS, column_count, features))
        windows = piece.reshape(4, 4, TILE_ROWS, GRID_COLS, TILE_COLS, features).transpose(3, 0, 1, 2, 4, 5).reshape(GRID_COLS, 4, window_tokens, features)
        frames = (time_block * 4 + 2 + jnp.arange(4, dtype=jnp.int32)) % frame_count
        rows = (row_block * TILE_ROWS + TILE_ROWS // 2 + jnp.arange(TILE_ROWS, dtype=jnp.int32)) % row_count
        cols = (jnp.arange(column_count, dtype=jnp.int32) + TILE_COLS // 2) % column_count
        frame_id, row_id, col_id = window_ids(frames, rows, cols)
        frame_tag = arrange(frame_id[:, None, None])
        row_tag = arrange(row_id[None, :, None])
        col_tag = arrange(col_id[None, None, :])
        usable = (frame_tag[:, :, None] == frame_tag[:, None, :]) & (row_tag[:, :, None] == row_tag[:, None, :]) & (col_tag[:, :, None] == col_tag[:, None, :])
        results = jax.vmap(window_attention)((windows[:, 0], windows[:, 1], windows[:, 2], windows[:, 3], usable))
        results = results.reshape(GRID_COLS, 4, 4, TILE_ROWS, TILE_COLS, features).transpose(1, 2, 3, 0, 4, 5)
        return results.reshape(4, 4, TILE_ROWS, column_count, features)
    gathered = lax.map(block, jnp.arange(time_blocks * grid_rows, dtype=jnp.int32))
    gathered = gathered.reshape(time_blocks, grid_rows, 4, 4, TILE_ROWS, column_count, features).transpose(2, 0, 3, 1, 4, 5, 6)
    whole = jnp.roll(gathered.reshape(4, frame_count, row_count, column_count, features), (2, TILE_ROWS // 2, TILE_COLS // 2), axis=(1, 2, 3))
    attn_out = whole[0]
    grad_normed_query = whole[1].astype(jnp.float32)
    grad_normed_key = whole[2].astype(jnp.float32)
    value_grad = whole[3]
    scaled_query = norm_gains[0] * grad_normed_query
    query_grad = (query_scale * scaled_query - query_full * query_scale ** 3 * lax.optimization_barrier(jnp.mean(query_full * scaled_query, axis=-1, keepdims=True))).astype(jnp.bfloat16)
    scaled_key = norm_gains[1] * grad_normed_key
    key_grad = (key_scale * scaled_key - key_full * key_scale ** 3 * lax.optimization_barrier(jnp.mean(key_full * scaled_key, axis=-1, keepdims=True))).astype(jnp.bfloat16)
    gain_grads = jnp.stack([lax.optimization_barrier(jnp.sum(grad_normed_query * query_full * query_scale, axis=(0, 1, 2))), lax.optimization_barrier(jnp.sum(grad_normed_key * key_full * key_scale, axis=(0, 1, 2)))])
    return (to_tiles(attn_out), to_tiles(query_grad), to_tiles(key_grad), to_tiles(value_grad), gain_grads)
```

```python
import functools

import jax
import jax.numpy as jnp
from jax import lax
from jax.experimental import pallas as pl
from jax.experimental.pallas import tpu as pltpu
from jax.sharding import PartitionSpec as P

HEADS = 20
HDIM = 128
EPSILON = 1e-06
GRID_COLS = 4
GRID_ROWS = 16
TIMES = 4
CHUNK = 4
CHUNKS = HEADS // CHUNK
OCT = 20
TOKENS = 8 * OCT
BLOCK = 4 * CHUNK * OCT
ROOT = HDIM ** (-0.5)
MESH = pl.DeviceIdType.MESH
F32 = jnp.float32
BF16 = jnp.bfloat16


def place():
    t = lax.axis_index("tm")
    s = lax.axis_index("space")
    return t, s // GRID_COLS, s % GRID_COLS


def shifted(where, bits, sign):
    t, r, c = where
    t = (t + sign * (bits // 4) + TIMES) % TIMES
    r = (r + sign * (bits // 2 % 2) + GRID_ROWS) % GRID_ROWS
    c = (c + sign * (bits % 2) + GRID_COLS) % GRID_COLS
    return (t, r * GRID_COLS + c)


def dot_nt(a, b):
    return lax.dot_general(a, b, (((1,), (1,)), ((), ())), preferred_element_type=F32)


def dot_nn(a, b):
    return lax.dot_general(a, b, (((1,), (0,)), ((), ())), preferred_element_type=F32)


def dot_tn(a, b):
    return lax.dot_general(a, b, (((0,), (0,)), ((), ())), preferred_element_type=F32)


def head_attention(q, k, v, g, bias):
    scores = dot_nt(q, k) * ROOT + bias
    highest = jnp.max(scores, axis=-1, keepdims=True)
    weights = jnp.exp(scores - highest)
    probs_full = weights / jnp.sum(weights, axis=-1, keepdims=True)
    probs = probs_full.astype(BF16)
    out = dot_nn(probs, v).astype(BF16)
    delta = jnp.sum(g.astype(F32) * out.astype(F32), axis=-1, keepdims=True)
    ds = (probs_full * (dot_nt(g, v) - delta) * ROOT).astype(BF16)
    dq = dot_nn(ds, k)
    dk = dot_tn(ds, q)
    dv = dot_tn(probs, g)
    return out.astype(F32), dq, dk, dv


def window_kernel(x_ref, out_ref, gain_ref, recv, res, bias, stage, fsend, frecv, bsend, brecv, own_sem):
    where = place()
    barrier = pltpu.get_barrier_semaphore()
    for bits in range(1, 8):
        for sign in (-1, 1):
            pl.semaphore_signal(barrier, inc=1, device_id=shifted(where, bits, sign), device_id_type=MESH)

    owner = lax.broadcasted_iota(jnp.int32, (TOKENS, TOKENS), 0)
    other = lax.broadcasted_iota(jnp.int32, (TOKENS, TOKENS), 1)
    differs = ((owner * 3277) >> 16) ^ ((other * 3277) >> 16)
    t, r, c = where
    cut = (
        jnp.where(t == TIMES - 1, 4, 0)
        + jnp.where(r == GRID_ROWS - 1, 2, 0)
        + jnp.where(c == GRID_COLS - 1, 1, 0)
    )
    bias[...] = jnp.where((differs & cut) == 0, 0.0, -1e30)

    def own_copy(g):
        return pltpu.make_async_copy(x_ref.at[7, g], recv.at[0, g], own_sem.at[g])

    def own_back(g):
        return pltpu.make_async_copy(res.at[0, g], out_ref.at[7, g], own_sem.at[g])

    def forth(g, bits):
        return pltpu.make_async_remote_copy(
            src_ref=x_ref.at[7 - bits, g],
            dst_ref=recv.at[bits, g],
            send_sem=fsend.at[g, bits],
            recv_sem=frecv.at[g, bits],
            device_id=shifted(where, bits, -1),
            device_id_type=MESH,
        )

    def back(g, bits):
        return pltpu.make_async_remote_copy(
            src_ref=res.at[bits, g],
            dst_ref=out_ref.at[7 - bits, g],
            send_sem=bsend.at[g, bits],
            recv_sem=brecv.at[g, bits],
            device_id=shifted(where, bits, 1),
            device_id_type=MESH,
        )

    pl.semaphore_wait(barrier, 14)

    @pl.loop(0, CHUNKS)
    def _(g):
        for bits in (2, 3, 6, 7, 1, 5, 4):
            forth(g, bits).start()
        own_copy(g).start()

    @pl.loop(0, CHUNKS)
    def _(g):
        own_copy(g).wait()
        for bits in range(1, 8):
            forth(g, bits).wait_recv()
        parts = CHUNK * OCT
        loaded = [
            [recv[bits, g, a * parts:(a + 1) * parts, :].astype(F32) for bits in range(8)]
            for a in range(4)
        ]
        for h in range(CHUNK):
            rows = slice(h * OCT, (h + 1) * OCT)
            q, k, v, og = [
                jnp.concatenate([loaded[a][bits][rows] for bits in range(8)], axis=0).astype(BF16)
                for a in range(4)
            ]
            results = head_attention(q, k, v, og, bias[...])
            for a in range(4):
                for bits in range(8):
                    stage[a, bits, rows, :] = results[a][bits * OCT:(bits + 1) * OCT]
            dq = results[1].astype(BF16).astype(F32) * q.astype(F32)
            dk = results[2].astype(BF16).astype(F32) * k.astype(F32)
            gain_ref[0, g, h:h + 1, :] = jnp.sum(dq, axis=0, keepdims=True)
            gain_ref[1, g, h:h + 1, :] = jnp.sum(dk, axis=0, keepdims=True)
        for bits in range(8):
            for a in range(4):
                res[bits, g, a * parts:(a + 1) * parts, :] = stage[a, bits].astype(BF16)
        for bits in (2, 3, 6, 7, 1, 5, 4):
            back(g, bits).start()
        own_back(g).start()

    @pl.loop(0, CHUNKS)
    def _(g):
        own_back(g).wait()
        for bits in range(1, 8):
            forth(g, bits).wait_send()
            back(g, bits).wait_send()
            back(g, bits).wait_recv()


def windows(x):
    block = (8, CHUNKS, BLOCK, HDIM)
    return pl.pallas_call(
        window_kernel,
        out_shape=(
            jax.ShapeDtypeStruct(block, BF16),
            jax.ShapeDtypeStruct((2, CHUNKS, CHUNK, HDIM), F32),
        ),
        in_specs=[pl.BlockSpec(memory_space=pl.ANY)],
        out_specs=(pl.BlockSpec(memory_space=pl.ANY), pl.BlockSpec(memory_space=pltpu.VMEM)),
        scratch_shapes=[
            pltpu.VMEM(block, BF16),
            pltpu.VMEM(block, BF16),
            pltpu.VMEM((TOKENS, TOKENS), F32),
            pltpu.VMEM((4, 8, CHUNK * OCT, HDIM), F32),
            pltpu.SemaphoreType.DMA((CHUNKS, 8)),
            pltpu.SemaphoreType.DMA((CHUNKS, 8)),
            pltpu.SemaphoreType.DMA((CHUNKS, 8)),
            pltpu.SemaphoreType.DMA((CHUNKS, 8)),
            pltpu.SemaphoreType.DMA((CHUNKS,)),
        ],
        compiler_params=pltpu.CompilerParams(
            collective_id=0, has_side_effects=True, vmem_limit_bytes=40 * 1024 * 1024
        ),
        name="windows",
    )(x)


def peers(where):
    t, r, c = where
    space = r * GRID_COLS + c
    z, xy = space % 8, space // 8
    along_t = [((t + i) % TIMES, space) for i in range(1, TIMES)]
    along_z = [(t, xy * 8 + (z + i) % 8) for i in range(1, 8)]
    along_xy = [(t, (xy + i) % 8 * 8 + z) for i in range(1, 8)]
    return along_t, along_z, along_xy


def reduce_kernel(g_ref, out_ref, held, slots, send_sem, recv_sem):
    rounds = peers(place())
    barrier = pltpu.get_barrier_semaphore()
    for group in rounds:
        for device in group:
            pl.semaphore_signal(barrier, inc=1, device_id=device, device_id_type=MESH)
    pl.semaphore_wait(barrier, 17)
    held[0] = g_ref[...]
    base = 0
    for step, group in enumerate(rounds):
        copies = []
        for i, device in enumerate(group):
            copies.append(
                pltpu.make_async_remote_copy(
                    src_ref=held.at[step],
                    dst_ref=slots.at[base + i],
                    send_sem=send_sem.at[base + i],
                    recv_sem=recv_sem.at[base + i],
                    device_id=device,
                    device_id_type=MESH,
                )
            )
        for copy in copies:
            copy.start()
        total = held[step]
        for i, copy in enumerate(copies):
            copy.wait()
            total = total + slots[base + i]
        if step < 2:
            held[step + 1] = total
        else:
            out_ref[...] = total
        base += len(group)


def reduced(gains):
    shape = (2 * HEADS, HDIM)
    return pl.pallas_call(
        reduce_kernel,
        out_shape=jax.ShapeDtypeStruct(shape, F32),
        in_specs=[pl.BlockSpec(memory_space=pltpu.VMEM)],
        out_specs=pl.BlockSpec(memory_space=pltpu.VMEM),
        scratch_shapes=[
            pltpu.VMEM((3,) + shape, F32),
            pltpu.VMEM((17,) + shape, F32),
            pltpu.SemaphoreType.DMA((17,)),
            pltpu.SemaphoreType.DMA((17,)),
        ],
        compiler_params=pltpu.CompilerParams(collective_id=1, has_side_effects=True),
        name="reduced",
    )(gains)


def rms_scale(values):
    return lax.rsqrt(jnp.mean(values * values, axis=-1, keepdims=True) + EPSILON)


def to_blocks(values):
    arranged = values.reshape(2, 2, 2, 2, 10, CHUNKS, CHUNK, HDIM)
    return arranged.transpose(0, 2, 3, 5, 6, 1, 4, 7)


def from_blocks(blocks):
    return blocks.reshape(2, 2, 2, CHUNKS, CHUNK, 2, 10, HDIM).transpose(0, 5, 1, 2, 6, 3, 4, 7).reshape(4, 2, 20, HEADS * HDIM)


def per_device(query_in, key_in, value_in, out_grad, norm_gains):
    query_in = query_in[:, 0]
    key_in = key_in[:, 0]
    value_in = value_in[:, 0]
    out_grad = out_grad[:, 0]
    query_full = query_in.astype(F32)
    key_full = key_in.astype(F32)
    query_scale = rms_scale(query_full)
    key_scale = rms_scale(key_full)
    normed_query = (query_full * query_scale * norm_gains[0]).astype(BF16)
    normed_key = (key_full * key_scale * norm_gains[1]).astype(BF16)
    packed = jnp.stack(
        [to_blocks(normed_query), to_blocks(normed_key), to_blocks(value_in), to_blocks(out_grad)],
        axis=4,
    )
    results, gains = windows(packed.reshape(8, CHUNKS, BLOCK, HDIM))
    total = reduced(gains.reshape(2 * HEADS, HDIM)).reshape(2, HEADS * HDIM) / norm_gains
    gain_grads = lax.dynamic_slice_in_dim(total, lax.axis_index("space") * 40, 40, axis=1)
    results = results.reshape(8, CHUNKS, 4, CHUNK, OCT, HDIM)
    attn_out, dq, dk, value_grad = [from_blocks(results[:, :, a]) for a in range(4)]
    scaled_query = norm_gains[0] * dq.astype(F32)
    query_grad = (
        query_scale * scaled_query
        - query_full * query_scale**3 * jnp.mean(query_full * scaled_query, axis=-1, keepdims=True)
    ).astype(BF16)
    scaled_key = norm_gains[1] * dk.astype(F32)
    key_grad = (
        key_scale * scaled_key
        - key_full * key_scale**3 * jnp.mean(key_full * scaled_key, axis=-1, keepdims=True)
    ).astype(BF16)
    return (
        attn_out[:, None],
        query_grad[:, None],
        key_grad[:, None],
        value_grad[:, None],
        gain_grads,
    )


def solution(mesh):
    token = P("tm", "space", None, None, None)
    return jax.shard_map(
        per_device,
        mesh=mesh,
        in_specs=(token, token, token, token, P()),
        out_specs=(token, token, token, token, P(None, "space")),
        check_vma=False,
    )
```

```python
import jax
import jax.numpy as jnp
from jax import lax
from jax.experimental import pallas as pl
from jax.experimental.pallas import tpu as pltpu
from jax.sharding import PartitionSpec as P

HEADS = 20
HDIM = 128
FEATURES = HEADS * HDIM
EPSILON = 1e-06
GRID_COLS = 4
GRID_ROWS = 16
TIMES = 4
CHUNK = 4
CHUNKS = HEADS // CHUNK
WIDTH = CHUNK * HDIM
HALF = 10
OCT = 2 * HALF
TOKENS = 8 * OCT
PART = CHUNK * OCT
BLOCK = 4 * PART
ROOT = HDIM ** (-0.5)
MESH = pl.DeviceIdType.MESH
F32 = jnp.float32
BF16 = jnp.bfloat16
FAR_FIRST = (2, 3, 6, 7, 1, 5, 4)


def shifted(where, bits, sign):
    t, r, c = where
    t = (t + sign * (bits // 4) + TIMES) % TIMES
    r = (r + sign * (bits // 2 % 2) + GRID_ROWS) % GRID_ROWS
    c = (c + sign * (bits % 2) + GRID_COLS) % GRID_COLS
    return (t, r * GRID_COLS + c)


def gain_peers(where):
    t, r, c = where
    space = r * GRID_COLS + c
    z, xy = space % 8, space // 8
    along_t = [((t + i) % TIMES, space) for i in range(1, TIMES)]
    along_z = [(t, xy * 8 + (z + i) % 8) for i in range(1, 8)]
    along_xy = [(t, (xy + i) % 8 * 8 + z) for i in range(1, 8)]
    return along_t, along_z, along_xy


def dot_nt(a, b):
    return lax.dot_general(a, b, (((1,), (1,)), ((), ())), preferred_element_type=F32)


def dot_nn(a, b):
    return lax.dot_general(a, b, (((1,), (0,)), ((), ())), preferred_element_type=F32)


def dot_tn(a, b):
    return lax.dot_general(a, b, (((0,), (0,)), ((), ())), preferred_element_type=F32)


def head_attention(q, k, v, g, bias):
    scores = dot_nt(q, k) * ROOT + bias
    highest = jnp.max(scores, axis=-1, keepdims=True)
    weights = jnp.exp(scores - highest)
    probs_full = weights / jnp.sum(weights, axis=-1, keepdims=True)
    probs = probs_full.astype(BF16)
    out = dot_nn(probs, v).astype(BF16)
    delta = jnp.sum(g.astype(F32) * out.astype(F32), axis=-1, keepdims=True)
    ds = (probs_full * (dot_nt(g, v) - delta) * ROOT).astype(BF16)
    dq = dot_nn(ds, k)
    dk = dot_tn(ds, q)
    dv = dot_tn(probs, g)
    return out.astype(F32), dq, dk, dv


def window_kernel(
    q_ref, k_ref, v_ref, g_ref, gain_ref, gain_rows_ref,
    out_ref, dq_ref, dk_ref, dv_ref, gains_out_ref,
    scale, dots, sent, recv, res, ret, bias, stage, held, slots, total_ref,
    fsend, frecv, bsend, brecv, own_sem, gsend, grecv,
):
    where = (
        lax.axis_index("tm"),
        lax.axis_index("space") // GRID_COLS,
        lax.axis_index("space") % GRID_COLS,
    )
    rounds = gain_peers(where)
    barrier = pltpu.get_barrier_semaphore()
    for bits in range(1, 8):
        for sign in (-1, 1):
            pl.semaphore_signal(barrier, inc=1, device_id=shifted(where, bits, sign), device_id_type=MESH)
    for group in rounds:
        for device in group:
            pl.semaphore_signal(barrier, inc=1, device_id=device, device_id_type=MESH)

    def own_copy(g):
        return pltpu.make_async_copy(sent.at[7, g], recv.at[0, g], own_sem.at[0, g])

    def own_back(g):
        return pltpu.make_async_copy(res.at[0, g], ret.at[7, g], own_sem.at[1, g])

    def forth(g, bits):
        return pltpu.make_async_remote_copy(
            src_ref=sent.at[7 - bits, g],
            dst_ref=recv.at[bits, g],
            send_sem=fsend.at[g, bits],
            recv_sem=frecv.at[g, bits],
            device_id=shifted(where, bits, -1),
            device_id_type=MESH,
        )

    def back(g, bits):
        return pltpu.make_async_remote_copy(
            src_ref=res.at[bits, g],
            dst_ref=ret.at[7 - bits, g],
            send_sem=bsend.at[g, bits],
            recv_sem=brecv.at[g, bits],
            device_id=shifted(where, bits, 1),
            device_id_type=MESH,
        )

    def gain_copies(step):
        base = (0, 3, 10)[step]
        return [
            pltpu.make_async_remote_copy(
                src_ref=held.at[step],
                dst_ref=slots.at[base + i],
                send_sem=gsend.at[base + i],
                recv_sem=grecv.at[base + i],
                device_id=device,
                device_id_type=MESH,
            )
            for i, device in enumerate(rounds[step])
        ]

    def gain_start(step):
        for copy in gain_copies(step):
            copy.start()

    def gain_finish(step):
        base = (0, 3, 10)[step]
        total = held[step]
        for i, copy in enumerate(gain_copies(step)):
            copy.wait()
            total = total + slots[base + i]
        return total

    @pl.loop(0, 8)
    def _(i):
        f, row = i // 2, i % 2
        for a, ref in ((0, q_ref), (1, k_ref)):
            x = ref[f, row].astype(F32)
            r = lax.rsqrt(jnp.mean(x * x, axis=-1, keepdims=True) + EPSILON)
            scale[a, i] = jnp.broadcast_to(r, (2 * HALF, HDIM))

    def cut_block(g, i):
        fh, row = i // 2, i % 2
        lanes = pl.ds(pl.multiple_of(g * WIDTH, WIDTH), WIDTH)
        for a, ref in enumerate((q_ref, k_ref, v_ref, g_ref)):
            frames = []
            for f in range(2):
                x = ref[2 * fh + f, row, :, lanes].astype(F32)
                heads = [x[:, h * HDIM:(h + 1) * HDIM] for h in range(CHUNK)]
                if a < 2:
                    r = scale[a, (2 * fh + f) * 2 + row]
                    heads = [
                        heads[h] * r * gain_ref[a * HEADS + g * CHUNK + h] for h in range(CHUNK)
                    ]
                frames.append(heads)
            for ch in range(2):
                cols = slice(ch * HALF, (ch + 1) * HALF)
                pieces = [frames[f][h][cols] for h in range(CHUNK) for f in range(2)]
                sent[i * 2 + ch, g, a * PART:(a + 1) * PART, :] = jnp.concatenate(pieces, axis=0).astype(BF16)

    owner = lax.broadcasted_iota(jnp.int32, (TOKENS, TOKENS), 0)
    other = lax.broadcasted_iota(jnp.int32, (TOKENS, TOKENS), 1)
    differs = ((owner * 3277) >> 16) ^ ((other * 3277) >> 16)
    t, r, c = where
    edge = (
        jnp.where(t == TIMES - 1, 4, 0)
        + jnp.where(r == GRID_ROWS - 1, 2, 0)
        + jnp.where(c == GRID_COLS - 1, 1, 0)
    )
    bias[...] = jnp.where((differs & edge) == 0, 0.0, -1e30)

    @pl.loop(0, 4)
    def _(i):
        cut_block(0, i)

    pl.semaphore_wait(barrier, 31)

    @pl.loop(0, CHUNKS)
    def _(g):
        for bits in FAR_FIRST:
            forth(g, bits).start()
        own_copy(g).start()

        @pl.when(g < CHUNKS - 1)
        def _():
            @pl.loop(0, 4)
            def _(i):
                cut_block(g + 1, i)

    @pl.loop(0, CHUNKS)
    def _(g):
        own_copy(g).wait()
        for bits in range(1, 8):
            forth(g, bits).wait_recv()
        loaded = [
            [recv[bits, g, a * PART:(a + 1) * PART, :].astype(F32) for bits in range(8)]
            for a in range(4)
        ]
        for h in range(CHUNK):
            rows = slice(h * OCT, (h + 1) * OCT)
            q, k, v, og = [
                jnp.concatenate([loaded[a][bits][rows] for bits in range(8)], axis=0).astype(BF16)
                for a in range(4)
            ]
            results = head_attention(q, k, v, og, bias[...])
            for a in range(4):
                for bits in range(8):
                    stage[a, bits, rows, :] = results[a][bits * OCT:(bits + 1) * OCT]
            dq = results[1].astype(BF16).astype(F32) * q.astype(F32)
            dk = results[2].astype(BF16).astype(F32) * k.astype(F32)
            held[0, pl.ds(g * CHUNK + h, 1), :] = jnp.sum(dq, axis=0, keepdims=True)
            held[0, pl.ds(HEADS + g * CHUNK + h, 1), :] = jnp.sum(dk, axis=0, keepdims=True)
        for bits in range(8):
            for a in range(4):
                res[bits, g, a * PART:(a + 1) * PART, :] = stage[a, bits].astype(BF16)

        @pl.when(g == CHUNKS - 1)
        def _():
            gain_start(0)

        for bits in FAR_FIRST:
            back(g, bits).start()
        own_back(g).start()

    dots[...] = jnp.zeros_like(dots)

    def join_block(g, i):
        fh, row = i // 2, i % 2
        lanes = pl.ds(pl.multiple_of(g * WIDTH, WIDTH), WIDTH)
        for a, ref in enumerate((out_ref, dq_ref, dk_ref, dv_ref)):
            sides = [ret[i * 2 + ch, g, a * PART:(a + 1) * PART, :].astype(F32) for ch in range(2)]
            for f in range(2):
                heads = []
                for h in range(CHUNK):
                    rows = slice(h * OCT + f * HALF, h * OCT + (f + 1) * HALF)
                    heads.append(jnp.concatenate([sides[0][rows], sides[1][rows]], axis=0))
                ref[2 * fh + f, row, :, lanes] = jnp.concatenate(heads, axis=1).astype(BF16)
                if a == 1 or a == 2:
                    x = (q_ref, k_ref)[a - 1][2 * fh + f, row, :, lanes].astype(F32)
                    total = dots[a - 1, (2 * fh + f) * 2 + row]
                    for h in range(CHUNK):
                        scaled = heads[h] * gain_ref[(a - 1) * HEADS + g * CHUNK + h]
                        total = total + scaled * x[:, h * HDIM:(h + 1) * HDIM]
                    dots[a - 1, (2 * fh + f) * 2 + row] = total

    @pl.loop(0, CHUNKS)
    def _(g):
        own_back(g).wait()
        for bits in range(1, 8):
            back(g, bits).wait_recv()

        @pl.loop(0, 4)
        def _(i):
            join_block(g, i)

        @pl.when(g == 0)
        def _():
            held[1] = gain_finish(0)
            gain_start(1)

        @pl.when(g == 2)
        def _():
            held[2] = gain_finish(1)
            gain_start(2)

    @pl.loop(0, 8)
    def _(i):
        f, row = i // 2, i % 2
        for a, x_ref, ref in ((0, q_ref, dq_ref), (1, k_ref, dk_ref)):
            r = scale[a, i]
            mean = jnp.sum(dots[a, i], axis=-1, keepdims=True) * (1.0 / FEATURES)
            factor = r * r * r * mean
            for h in range(HEADS):
                lanes = slice(h * HDIM, (h + 1) * HDIM)
                x = x_ref[f, row, :, lanes].astype(F32)
                scaled = ref[f, row, :, lanes].astype(F32) * gain_ref[a * HEADS + h]
                ref[f, row, :, lanes] = (r * scaled - x * factor).astype(BF16)

    total_ref[...] = gain_finish(2) / gain_rows_ref[...]
    first = lax.axis_index("space") * (FEATURES // 64)
    line = first // HDIM
    lane = first % HDIM
    back_by = (HDIM - lane) % HDIM
    place = lax.broadcasted_iota(jnp.int32, (1, HDIM), 1)
    for a in range(2):
        this = total_ref[pl.ds(a * HEADS + line, 1), :]
        following = total_ref[pl.ds(a * HEADS + (line + 1) % HEADS, 1), :]
        joined = jnp.where(
            place < HDIM - lane, pltpu.roll(this, back_by, 1), pltpu.roll(following, back_by, 1)
        )
        gains_out_ref[a:a + 1, :] = joined

    @pl.loop(0, CHUNKS)
    def _(g):
        for bits in range(1, 8):
            forth(g, bits).wait_send()
            back(g, bits).wait_send()


def windows(query, key, value, grad, gains):
    block = (8, CHUNKS, BLOCK, HDIM)
    natural = jax.ShapeDtypeStruct(query.shape, BF16)
    vmem = pl.BlockSpec(memory_space=pltpu.VMEM)
    return pl.pallas_call(
        window_kernel,
        out_shape=(natural,) * 4 + (jax.ShapeDtypeStruct((2, HDIM), F32),),
        in_specs=[vmem] * 6,
        out_specs=(vmem,) * 5,
        scratch_shapes=[
            pltpu.VMEM((2, 8, 2 * HALF, HDIM), F32),
            pltpu.VMEM((2, 8, 2 * HALF, HDIM), F32),
            pltpu.VMEM(block, BF16),
            pltpu.VMEM(block, BF16),
            pltpu.VMEM(block, BF16),
            pltpu.VMEM(block, BF16),
            pltpu.VMEM((TOKENS, TOKENS), F32),
            pltpu.VMEM((4, 8, PART, HDIM), F32),
            pltpu.VMEM((3, 2 * HEADS, HDIM), F32),
            pltpu.VMEM((17, 2 * HEADS, HDIM), F32),
            pltpu.VMEM((2 * HEADS, HDIM), F32),
            pltpu.SemaphoreType.DMA((CHUNKS, 8)),
            pltpu.SemaphoreType.DMA((CHUNKS, 8)),
            pltpu.SemaphoreType.DMA((CHUNKS, 8)),
            pltpu.SemaphoreType.DMA((CHUNKS, 8)),
            pltpu.SemaphoreType.DMA((2, CHUNKS)),
            pltpu.SemaphoreType.DMA((17,)),
            pltpu.SemaphoreType.DMA((17,)),
        ],
        compiler_params=pltpu.CompilerParams(
            collective_id=0, has_side_effects=True, vmem_limit_bytes=48 * 1024 * 1024
        ),
        name="windows",
    )(query, key, value, grad, gains.reshape(2 * HEADS, 1, HDIM), gains.reshape(2 * HEADS, HDIM))


def per_device(query_in, key_in, value_in, out_grad, norm_gains):
    outs = windows(query_in[:, 0], key_in[:, 0], value_in[:, 0], out_grad[:, 0], norm_gains)
    return tuple(out[:, None] for out in outs[:4]) + (outs[4][:, :FEATURES // 64],)


def solution(mesh):
    token = P("tm", "space", None, None, None)
    return jax.shard_map(
        per_device,
        mesh=mesh,
        in_specs=(token, token, token, token, P()),
        out_specs=(token, token, token, token, P(None, "space")),
        check_vma=False,
    )
```

```python
import jax
import jax.numpy as jnp
from jax import lax
from jax.experimental import pallas as pl
from jax.experimental.pallas import tpu as pltpu
from jax.sharding import PartitionSpec as P

HEADS = 20
HDIM = 128
FEATURES = HEADS * HDIM
EPSILON = 1e-06
GRID_COLS = 4
GRID_ROWS = 16
TIMES = 4
CHUNK = 4
CHUNKS = HEADS // CHUNK
WIDTH = CHUNK * HDIM
COLS = 20
HALF = 10
PLACES = 2 * COLS
TOKENS = 160
MAIN = 16
REST = 4
PART = CHUNK * (MAIN + REST)
BLOCK = 4 * PART
ROOT = HDIM ** (-0.5)
MESH = pl.DeviceIdType.MESH
F32 = jnp.float32
BF16 = jnp.bfloat16
FAR_FIRST = (2, 3, 6, 7, 1, 5, 4)


def shifted(where, bits, sign):
    t, r, c = where
    t = (t + sign * (bits // 4) + TIMES) % TIMES
    r = (r + sign * (bits // 2 % 2) + GRID_ROWS) % GRID_ROWS
    c = (c + sign * (bits % 2) + GRID_COLS) % GRID_COLS
    return (t, r * GRID_COLS + c)


def gain_peers(where):
    t, r, c = where
    space = r * GRID_COLS + c
    z, xy = space % 8, space // 8
    along_t = [((t + i) % TIMES, space) for i in range(1, TIMES)]
    along_z = [(t, xy * 8 + (z + i) % 8) for i in range(1, 8)]
    along_xy = [(t, (xy + i) % 8 * 8 + z) for i in range(1, 8)]
    return along_t, along_z, along_xy


def dot_nt(a, b):
    return lax.dot_general(a, b, (((1,), (1,)), ((), ())), preferred_element_type=F32)


def dot_nn(a, b):
    return lax.dot_general(a, b, (((1,), (0,)), ((), ())), preferred_element_type=F32)


def dot_tn(a, b):
    return lax.dot_general(a, b, (((0,), (0,)), ((), ())), preferred_element_type=F32)


def head_attention(q, k, v, g, bias):
    scores = dot_nt(q, k) * ROOT + bias
    highest = jnp.max(scores, axis=-1, keepdims=True)
    weights = jnp.exp(scores - highest)
    probs_full = weights / jnp.sum(weights, axis=-1, keepdims=True)
    probs = probs_full.astype(BF16)
    out = dot_nn(probs, v).astype(BF16)
    delta = jnp.sum(g.astype(F32) * out.astype(F32), axis=-1, keepdims=True)
    ds = (probs_full * (dot_nt(g, v) - delta) * ROOT).astype(BF16)
    dq = dot_nn(ds, k)
    dk = dot_tn(ds, q)
    dv = dot_tn(probs, g)
    return out.astype(F32), dq, dk, dv


def lanes_of(head):
    return pl.ds(pl.multiple_of(head * HDIM, HDIM), HDIM)


def flat(ref, f, lanes):
    return ref[f, :, :, lanes].reshape(PLACES, HDIM).astype(F32)


def put_flat(ref, f, lanes, value):
    ref[f, :, :, lanes] = value.astype(BF16).reshape(COLS, 2, HDIM)


def norm_scales(q_ref, k_ref, scale):
    @pl.loop(0, 4)
    def _(f):
        for a, ref in ((0, q_ref), (1, k_ref)):
            total = jnp.zeros((PLACES, HDIM), F32)
            for h in range(HEADS):
                x = flat(ref, f, pl.ds(h * HDIM, HDIM))
                total = total + x * x
            mean = jnp.sum(total, axis=-1, keepdims=True) * (1.0 / FEATURES)
            scale[a, f] = jnp.broadcast_to(lax.rsqrt(mean + EPSILON), (PLACES, HDIM))


def cut_block(g, fh, refs, gain_ref, scale, rows, sent):
    for a, ref in enumerate(refs):
        for f in range(2):
            for h in range(CHUNK):
                lanes = lanes_of(g * CHUNK + h)
                x = flat(ref, 2 * fh + f, lanes)
                if a < 2:
                    x = x * scale[a, 2 * fh + f] * gain_ref[a:a + 1, lanes]
                rows[(a * 2 + f) * CHUNK + h] = x
        for row in range(2):
            for ch in range(2):
                start = row + 2 * HALF * ch
                main = []
                rest = []
                for h in range(CHUNK):
                    for f in range(2):
                        i = (a * 2 + f) * CHUNK + h
                        main.append(rows[i, pl.ds(start, 8, stride=2), :])
                        rest.append(rows[i, pl.ds(start + 16, 2, stride=2), :])
                block = jnp.concatenate(main + rest, axis=0).astype(BF16)
                sent[fh * 4 + row * 2 + ch, g, a * PART:(a + 1) * PART, :] = block


def join_block(g, fh, ret, refs, x_refs, gain_ref, rows, dots):
    for a, ref in enumerate(refs):
        for row in range(2):
            for ch in range(2):
                start = row + 2 * HALF * ch
                block = ret[fh * 4 + row * 2 + ch, g, a * PART:(a + 1) * PART, :].astype(F32)
                for h in range(CHUNK):
                    for f in range(2):
                        i = (a * 2 + f) * CHUNK + h
                        main = h * MAIN + f * 8
                        rest = CHUNK * MAIN + h * REST + f * 2
                        rows[i, pl.ds(start, 8, stride=2), :] = block[main:main + 8]
                        rows[i, pl.ds(start + 16, 2, stride=2), :] = block[rest:rest + 2]
        for f in range(2):
            total = dots[a - 1, 2 * fh + f] if a in (1, 2) else None
            for h in range(CHUNK):
                lanes = lanes_of(g * CHUNK + h)
                value = rows[(a * 2 + f) * CHUNK + h]
                put_flat(ref, 2 * fh + f, lanes, value)
                if a in (1, 2):
                    x = flat(x_refs[a - 1], 2 * fh + f, lanes)
                    total = total + value * gain_ref[a - 1:a, lanes] * x
            if a in (1, 2):
                dots[a - 1, 2 * fh + f] = total


def norm_backward(x_refs, refs, gain_ref, scale, dots):
    @pl.loop(0, 4)
    def _(f):
        for a in range(2):
            r = scale[a, f]
            mean = jnp.sum(dots[a, f], axis=-1, keepdims=True) * (1.0 / FEATURES)
            factor = r * r * r * mean
            for h in range(HEADS):
                lanes = pl.ds(h * HDIM, HDIM)
                scaled = flat(refs[a], f, lanes) * gain_ref[a:a + 1, lanes]
                put_flat(refs[a], f, lanes, r * scaled - flat(x_refs[a], f, lanes) * factor)


def window_mask(where, bias):
    owner = lax.broadcasted_iota(jnp.int32, (TOKENS, TOKENS), 0)
    other = lax.broadcasted_iota(jnp.int32, (TOKENS, TOKENS), 1)
    octants = [jnp.where(i < 8 * MAIN, i >> 4, (i - 8 * MAIN) >> 2) for i in (owner, other)]
    t, r, c = where
    edge = (
        jnp.where(t == TIMES - 1, 4, 0)
        + jnp.where(r == GRID_ROWS - 1, 2, 0)
        + jnp.where(c == GRID_COLS - 1, 1, 0)
    )
    bias[...] = jnp.where(((octants[0] ^ octants[1]) & edge) == 0, 0.0, -1e30)


def attend(g, recv, res, bias, stage, sums):
    ends = [
        [
            recv[bits, g, a * PART + CHUNK * MAIN:(a + 1) * PART, :].astype(F32)
            for bits in range(8)
        ]
        for a in range(4)
    ]
    for h in range(CHUNK):
        window = []
        for a in range(4):
            start = a * PART + h * MAIN
            mains = [recv[bits, g, start:start + MAIN, :] for bits in range(8)]
            rests = [ends[a][bits][h * REST:(h + 1) * REST] for bits in range(8)]
            window.append(jnp.concatenate(mains + [jnp.concatenate(rests, axis=0).astype(BF16)], axis=0))
        results = head_attention(*window, bias[...])
        for a in range(4):
            start = a * PART + h * MAIN
            for bits in range(8):
                res[bits, g, start:start + MAIN, :] = results[a][bits * MAIN:(bits + 1) * MAIN].astype(BF16)
                rest = 8 * MAIN + bits * REST
                stage[a, bits, h * REST:(h + 1) * REST, :] = results[a][rest:rest + REST]
        for a in range(2):
            terms = results[1 + a].astype(BF16).astype(F32) * window[a].astype(F32)
            sums[0, pl.ds(a * HEADS + g * CHUNK + h, 1), :] = jnp.sum(terms, axis=0, keepdims=True)
    for bits in range(8):
        for a in range(4):
            res[bits, g, a * PART + CHUNK * MAIN:(a + 1) * PART, :] = stage[a, bits].astype(BF16)


def window_kernel(
    q_ref, k_ref, v_ref, g_ref, gain_ref,
    out_ref, dq_ref, dk_ref, dv_ref, gains_out_ref,
    scale, dots, rows, sent, recv, res, ret, bias, stage, held, slots, total_ref,
    fsend, frecv, bsend, brecv, own_sem, gsend, grecv,
):
    where = (
        lax.axis_index("tm"),
        lax.axis_index("space") // GRID_COLS,
        lax.axis_index("space") % GRID_COLS,
    )
    rounds = gain_peers(where)
    barrier = pltpu.get_barrier_semaphore()
    for bits in range(1, 8):
        for sign in (-1, 1):
            pl.semaphore_signal(barrier, inc=1, device_id=shifted(where, bits, sign), device_id_type=MESH)
    for group in rounds:
        for device in group:
            pl.semaphore_signal(barrier, inc=1, device_id=device, device_id_type=MESH)

    def own_copy(g):
        return pltpu.make_async_copy(sent.at[7, g], recv.at[0, g], own_sem.at[0, g])

    def own_back(g):
        return pltpu.make_async_copy(res.at[0, g], ret.at[7, g], own_sem.at[1, g])

    def forth(g, bits):
        return pltpu.make_async_remote_copy(
            src_ref=sent.at[7 - bits, g],
            dst_ref=recv.at[bits, g],
            send_sem=fsend.at[g, bits],
            recv_sem=frecv.at[g, bits],
            device_id=shifted(where, bits, -1),
            device_id_type=MESH,
        )

    def back(g, bits):
        return pltpu.make_async_remote_copy(
            src_ref=res.at[bits, g],
            dst_ref=ret.at[7 - bits, g],
            send_sem=bsend.at[g, bits],
            recv_sem=brecv.at[g, bits],
            device_id=shifted(where, bits, 1),
            device_id_type=MESH,
        )

    def gain_copies(step):
        base = (0, 3, 10)[step]
        return [
            pltpu.make_async_remote_copy(
                src_ref=held.at[step],
                dst_ref=slots.at[base + i],
                send_sem=gsend.at[base + i],
                recv_sem=grecv.at[base + i],
                device_id=device,
                device_id_type=MESH,
            )
            for i, device in enumerate(rounds[step])
        ]

    def gain_start(step):
        for copy in gain_copies(step):
            copy.start()

    def gain_finish(step):
        base = (0, 3, 10)[step]
        total = held[step]
        for i, copy in enumerate(gain_copies(step)):
            copy.wait()
            total = total + slots[base + i]
        return total

    ins = (q_ref, k_ref, v_ref, g_ref)
    outs = (out_ref, dq_ref, dk_ref, dv_ref)
    norm_scales(q_ref, k_ref, scale)

    @pl.loop(0, 2)
    def _(fh):
        cut_block(0, fh, ins, gain_ref, scale, rows, sent)

    pl.semaphore_wait(barrier, 31)

    @pl.loop(0, CHUNKS)
    def _(g):
        for bits in FAR_FIRST:
            forth(g, bits).start()
        own_copy(g).start()

        @pl.when(g < CHUNKS - 1)
        def _():
            @pl.loop(0, 2)
            def _(fh):
                cut_block(g + 1, fh, ins, gain_ref, scale, rows, sent)

    window_mask(where, bias)

    @pl.loop(0, CHUNKS)
    def _(g):
        own_copy(g).wait()
        for bits in range(1, 8):
            forth(g, bits).wait_recv()
        attend(g, recv, res, bias, stage, held)

        @pl.when(g == CHUNKS - 1)
        def _():
            gain_start(0)

        for bits in FAR_FIRST:
            back(g, bits).start()
        own_back(g).start()

    dots[...] = jnp.zeros_like(dots)

    @pl.loop(0, CHUNKS)
    def _(g):
        own_back(g).wait()
        for bits in range(1, 8):
            back(g, bits).wait_recv()

        @pl.loop(0, 2)
        def _(fh):
            join_block(g, fh, ret, outs, ins, gain_ref, rows, dots)

        @pl.when(g == 0)
        def _():
            held[1] = gain_finish(0)
            gain_start(1)

        @pl.when(g == 2)
        def _():
            held[2] = gain_finish(1)
            gain_start(2)

    norm_backward(ins[:2], outs[1:3], gain_ref, scale, dots)

    total_ref[...] = gain_finish(2)
    width = FEATURES // 64
    first = lax.axis_index("space") * width
    line = first // HDIM
    lane = first % HDIM
    back_by = (HDIM - lane) % HDIM
    place = lax.broadcasted_iota(jnp.int32, (1, HDIM), 1)
    for a in range(2):
        parts = []
        for i in (line, (line + 1) % HEADS):
            mean = total_ref[pl.ds(a * HEADS + i, 1), :] / gain_ref[a:a + 1, lanes_of(i)]
            parts.append(pltpu.roll(mean, back_by, 1))
        joined = jnp.where(place < HDIM - lane, parts[0], parts[1])
        gains_out_ref[a:a + 1, :] = joined[:, :width]

    @pl.loop(0, CHUNKS)
    def _(g):
        for bits in range(1, 8):
            forth(g, bits).wait_send()
            back(g, bits).wait_send()


def windows(query, key, value, grad, gains):
    block = (8, CHUNKS, BLOCK, HDIM)
    natural = jax.ShapeDtypeStruct(query.shape, BF16)
    vmem = pl.BlockSpec(memory_space=pltpu.VMEM)
    return pl.pallas_call(
        window_kernel,
        out_shape=(natural,) * 4 + (jax.ShapeDtypeStruct((2, FEATURES // 64), F32),),
        in_specs=[vmem] * 5,
        out_specs=(vmem,) * 5,
        scratch_shapes=[
            pltpu.VMEM((2, 4, PLACES, HDIM), F32),
            pltpu.VMEM((2, 4, PLACES, HDIM), F32),
            pltpu.VMEM((8 * CHUNK, PLACES, HDIM), F32),
            pltpu.VMEM(block, BF16),
            pltpu.VMEM(block, BF16),
            pltpu.VMEM(block, BF16),
            pltpu.VMEM(block, BF16),
            pltpu.VMEM((TOKENS, TOKENS), F32),
            pltpu.VMEM((4, 8, CHUNK * REST, HDIM), F32),
            pltpu.VMEM((3, 2 * HEADS, HDIM), F32),
            pltpu.VMEM((17, 2 * HEADS, HDIM), F32),
            pltpu.VMEM((2 * HEADS, HDIM), F32),
            pltpu.SemaphoreType.DMA((CHUNKS, 8)),
            pltpu.SemaphoreType.DMA((CHUNKS, 8)),
            pltpu.SemaphoreType.DMA((CHUNKS, 8)),
            pltpu.SemaphoreType.DMA((CHUNKS, 8)),
            pltpu.SemaphoreType.DMA((2, CHUNKS)),
            pltpu.SemaphoreType.DMA((17,)),
            pltpu.SemaphoreType.DMA((17,)),
        ],
        compiler_params=pltpu.CompilerParams(
            collective_id=0, has_side_effects=True, vmem_limit_bytes=48 * 1024 * 1024
        ),
        name="windows",
    )(query, key, value, grad, gains)


def per_device(query_in, key_in, value_in, out_grad, norm_gains):
    tokens = [x[:, 0].transpose(0, 2, 1, 3) for x in (query_in, key_in, value_in, out_grad)]
    outs = windows(*tokens, norm_gains)
    return tuple(out.transpose(0, 2, 1, 3)[:, None] for out in outs[:4]) + (outs[4],)


def solution(mesh):
    token = P("tm", "space", None, None, None)
    return jax.shard_map(
        per_device,
        mesh=mesh,
        in_specs=(token, token, token, token, P()),
        out_specs=(token, token, token, token, P(None, "space")),
        check_vma=False,
    )
```

```python
import jax
import jax.numpy as jnp
from jax import lax
from jax.experimental import pallas as pl
from jax.experimental.pallas import tpu as pltpu
from jax.sharding import PartitionSpec as P

HEADS = 20
HDIM = 128
FEATURES = HEADS * HDIM
EPSILON = 1e-06
GRID_COLS = 4
GRID_ROWS = 16
TIMES = 4
CHUNK = 4
CHUNKS = HEADS // CHUNK
WIDTH = CHUNK * HDIM
COLS = 20
HALF = 10
PLACES = 2 * COLS
TOKENS = 160
MAIN = 16
REST = 4
PART = CHUNK * (MAIN + REST)
BLOCK = 4 * PART
ROOT = HDIM ** (-0.5)
MESH = pl.DeviceIdType.MESH
F32 = jnp.float32
BF16 = jnp.bfloat16
FAR_FIRST = (2, 3, 6, 7, 1, 5, 4)


def shifted(where, bits, sign):
    t, r, c = where
    t = (t + sign * (bits // 4) + TIMES) % TIMES
    r = (r + sign * (bits // 2 % 2) + GRID_ROWS) % GRID_ROWS
    c = (c + sign * (bits % 2) + GRID_COLS) % GRID_COLS
    return (t, r * GRID_COLS + c)


def gain_peers(where):
    t, r, c = where
    space = r * GRID_COLS + c
    z, xy = space % 8, space // 8
    along_t = [((t + i) % TIMES, space) for i in range(1, TIMES)]
    along_z = [(t, xy * 8 + (z + i) % 8) for i in range(1, 8)]
    along_xy = [(t, (xy + i) % 8 * 8 + z) for i in range(1, 8)]
    return along_t, along_z, along_xy


def dot_nt(a, b):
    return lax.dot_general(a, b, (((1,), (1,)), ((), ())), preferred_element_type=F32)


def dot_nn(a, b):
    return lax.dot_general(a, b, (((1,), (0,)), ((), ())), preferred_element_type=F32)


def dot_tn(a, b):
    return lax.dot_general(a, b, (((0,), (0,)), ((), ())), preferred_element_type=F32)


def head_attention(q, k, v, g, bias):
    scores = dot_nt(q, k) * ROOT + bias
    highest = jnp.max(scores, axis=-1, keepdims=True)
    weights = jnp.exp(scores - highest)
    probs_full = weights / jnp.sum(weights, axis=-1, keepdims=True)
    probs = probs_full.astype(BF16)
    out = dot_nn(probs, v).astype(BF16)
    delta = jnp.sum(g.astype(F32) * out.astype(F32), axis=-1, keepdims=True)
    ds = (probs_full * (dot_nt(g, v) - delta) * ROOT).astype(BF16)
    dq = dot_nn(ds, k)
    dk = dot_tn(ds, q)
    dv = dot_tn(probs, g)
    return out.astype(F32), dq, dk, dv


def lanes_of(head):
    return pl.ds(pl.multiple_of(head * HDIM, HDIM), HDIM)


def flat(ref, f, lanes):
    return ref[f, :, :, lanes].reshape(PLACES, HDIM).astype(F32)


def put_flat(ref, f, lanes, value):
    ref[f, :, :, lanes] = value.astype(BF16).reshape(COLS, 2, HDIM)


def norm_scales(refs, flat_x, scale):
    @pl.loop(0, 4)
    def _(f):
        for a, ref in enumerate(refs):
            total = jnp.zeros((PLACES, HDIM), F32)
            for h in range(HEADS):
                x = flat(ref, f, pl.ds(h * HDIM, HDIM))
                flat_x[a, f, h] = x
                total = total + x * x
            mean = jnp.sum(total, axis=-1, keepdims=True) * (1.0 / FEATURES)
            scale[a, f] = jnp.broadcast_to(lax.rsqrt(mean + EPSILON), (PLACES, HDIM))


def cut_block(arrays, g, fh, flat_x, refs, gain_ref, scale, rows, sent):
    for a in arrays:
        for f in range(2):
            for h in range(CHUNK):
                head = g * CHUNK + h
                if a < 2:
                    x = flat_x[a, 2 * fh + f, head] * scale[a, 2 * fh + f]
                    x = x * gain_ref[a:a + 1, lanes_of(head)]
                else:
                    x = flat(refs[a - 2], 2 * fh + f, lanes_of(head))
                rows[(a * 2 + f) * CHUNK + h] = x
        for row in range(2):
            for ch in range(2):
                start = row + 2 * HALF * ch
                main = []
                rest = []
                for h in range(CHUNK):
                    for f in range(2):
                        i = (a * 2 + f) * CHUNK + h
                        main.append(rows[i, pl.ds(start, 8, stride=2), :])
                        rest.append(rows[i, pl.ds(start + 16, 2, stride=2), :])
                block = jnp.concatenate(main + rest, axis=0).astype(BF16)
                sent[fh * 4 + row * 2 + ch, g, a * PART:(a + 1) * PART, :] = block


def join_block(g, fh, ret, out_ref, dv_ref, flat_x, flat_a, gain_ref, rows, scale, dots):
    for a in range(4):
        for row in range(2):
            for ch in range(2):
                start = row + 2 * HALF * ch
                block = ret[fh * 4 + row * 2 + ch, g, a * PART:(a + 1) * PART, :].astype(F32)
                for h in range(CHUNK):
                    for f in range(2):
                        i = (a * 2 + f) * CHUNK + h
                        main = h * MAIN + f * 8
                        rest = CHUNK * MAIN + h * REST + f * 2
                        rows[i, pl.ds(start, 8, stride=2), :] = block[main:main + 8]
                        rows[i, pl.ds(start + 16, 2, stride=2), :] = block[rest:rest + 2]
        for f in range(2):
            frame = 2 * fh + f
            total = dots[a - 1, frame] if a in (1, 2) else None
            for h in range(CHUNK):
                head = g * CHUNK + h
                value = rows[(a * 2 + f) * CHUNK + h]
                if a in (1, 2):
                    scaled = value * gain_ref[a - 1:a, lanes_of(head)]
                    flat_a[a - 1, frame, head] = scaled
                    total = total + scaled * flat_x[a - 1, frame, head]
                else:
                    put_flat((out_ref, dv_ref)[a // 3], frame, lanes_of(head), value)
            if a in (1, 2):
                dots[a - 1, frame] = total


def window_mask(where, bias):
    owner = lax.broadcasted_iota(jnp.int32, (TOKENS, TOKENS), 0)
    other = lax.broadcasted_iota(jnp.int32, (TOKENS, TOKENS), 1)
    octants = [jnp.where(i < 8 * MAIN, i >> 4, (i - 8 * MAIN) >> 2) for i in (owner, other)]
    t, r, c = where
    edge = (
        jnp.where(t == TIMES - 1, 4, 0)
        + jnp.where(r == GRID_ROWS - 1, 2, 0)
        + jnp.where(c == GRID_COLS - 1, 1, 0)
    )
    bias[...] = jnp.where(((octants[0] ^ octants[1]) & edge) == 0, 0.0, -1e30)


def attend(g, recv, res, bias, stage, sums):
    ends = [
        [
            recv[bits, g, a * PART + CHUNK * MAIN:(a + 1) * PART, :].astype(F32)
            for bits in range(8)
        ]
        for a in range(4)
    ]
    for h in range(CHUNK):
        window = []
        for a in range(4):
            start = a * PART + h * MAIN
            mains = [recv[bits, g, start:start + MAIN, :] for bits in range(8)]
            rests = [ends[a][bits][h * REST:(h + 1) * REST] for bits in range(8)]
            window.append(jnp.concatenate(mains + [jnp.concatenate(rests, axis=0).astype(BF16)], axis=0))
        results = head_attention(*window, bias[...])
        for a in range(4):
            start = a * PART + h * MAIN
            for bits in range(8):
                res[bits, g, start:start + MAIN, :] = results[a][bits * MAIN:(bits + 1) * MAIN].astype(BF16)
                rest = 8 * MAIN + bits * REST
                stage[a, bits, h * REST:(h + 1) * REST, :] = results[a][rest:rest + REST]
        for a in range(2):
            terms = results[1 + a].astype(BF16).astype(F32) * window[a].astype(F32)
            sums[0, pl.ds(a * HEADS + g * CHUNK + h, 1), :] = jnp.sum(terms, axis=0, keepdims=True)
    for bits in range(8):
        for a in range(4):
            res[bits, g, a * PART + CHUNK * MAIN:(a + 1) * PART, :] = stage[a, bits].astype(BF16)


def window_kernel(
    q_hbm, k_hbm, v_hbm, g_hbm, gain_hbm,
    out_ref, dv_ref, flat_x, flat_a, scale, dots, gains_out_ref,
    q_ref, k_ref, v_ref, g_ref, gain_ref,
    rows, sent, recv, res, ret, bias, stage, held, slots, total_ref,
    fsend, frecv, bsend, brecv, own_sem, gsend, grecv, in_sem,
):
    where = (
        lax.axis_index("tm"),
        lax.axis_index("space") // GRID_COLS,
        lax.axis_index("space") % GRID_COLS,
    )
    early = pl.ds(0, WIDTH)
    late = pl.ds(WIDTH, FEATURES - WIDTH)
    loads = [
        pltpu.make_async_copy(v_hbm.at[:, :, :, early], v_ref.at[:, :, :, early], in_sem.at[0]),
        pltpu.make_async_copy(g_hbm.at[:, :, :, early], g_ref.at[:, :, :, early], in_sem.at[1]),
        pltpu.make_async_copy(q_hbm, q_ref, in_sem.at[2]),
        pltpu.make_async_copy(k_hbm, k_ref, in_sem.at[3]),
        pltpu.make_async_copy(gain_hbm, gain_ref, in_sem.at[4]),
        pltpu.make_async_copy(v_hbm.at[:, :, :, late], v_ref.at[:, :, :, late], in_sem.at[5]),
        pltpu.make_async_copy(g_hbm.at[:, :, :, late], g_ref.at[:, :, :, late], in_sem.at[6]),
    ]
    for load in loads:
        load.start()

    rounds = gain_peers(where)
    barrier = pltpu.get_barrier_semaphore()
    for bits in range(1, 8):
        for sign in (-1, 1):
            pl.semaphore_signal(barrier, inc=1, device_id=shifted(where, bits, sign), device_id_type=MESH)
    for group in rounds:
        for device in group:
            pl.semaphore_signal(barrier, inc=1, device_id=device, device_id_type=MESH)

    def own_copy(g):
        return pltpu.make_async_copy(sent.at[7, g], recv.at[0, g], own_sem.at[0, g])

    def own_back(g):
        return pltpu.make_async_copy(res.at[0, g], ret.at[7, g], own_sem.at[1, g])

    def forth(g, bits):
        return pltpu.make_async_remote_copy(
            src_ref=sent.at[7 - bits, g],
            dst_ref=recv.at[bits, g],
            send_sem=fsend.at[g, bits],
            recv_sem=frecv.at[g, bits],
            device_id=shifted(where, bits, -1),
            device_id_type=MESH,
        )

    def forth_half(half, bits):
        part = pl.ds(half * 2 * PART, 2 * PART)
        sem = (CHUNKS, 0)[half]
        return pltpu.make_async_remote_copy(
            src_ref=sent.at[7 - bits, 0, part],
            dst_ref=recv.at[bits, 0, part],
            send_sem=fsend.at[sem, bits],
            recv_sem=frecv.at[sem, bits],
            device_id=shifted(where, bits, -1),
            device_id_type=MESH,
        )

    def back(g, bits):
        return pltpu.make_async_remote_copy(
            src_ref=res.at[bits, g],
            dst_ref=ret.at[7 - bits, g],
            send_sem=bsend.at[g, bits],
            recv_sem=brecv.at[g, bits],
            device_id=shifted(where, bits, 1),
            device_id_type=MESH,
        )

    def gain_copies(step):
        base = (0, 3, 10)[step]
        return [
            pltpu.make_async_remote_copy(
                src_ref=held.at[step],
                dst_ref=slots.at[base + i],
                send_sem=gsend.at[base + i],
                recv_sem=grecv.at[base + i],
                device_id=device,
                device_id_type=MESH,
            )
            for i, device in enumerate(rounds[step])
        ]

    def gain_start(step):
        for copy in gain_copies(step):
            copy.start()

    def gain_finish(step):
        base = (0, 3, 10)[step]
        total = held[step]
        for i, copy in enumerate(gain_copies(step)):
            copy.wait()
            total = total + slots[base + i]
        return total

    def cut(arrays, g):
        @pl.loop(0, 2)
        def _(fh):
            cut_block(arrays, g, fh, flat_x, (v_ref, g_ref), gain_ref, scale, rows, sent)

    loads[0].wait()
    loads[1].wait()
    cut((2, 3), 0)
    pl.semaphore_wait(barrier, 31)
    for bits in FAR_FIRST:
        forth_half(1, bits).start()
    for load in loads[2:5]:
        load.wait()
    norm_scales((q_ref, k_ref), flat_x, scale)
    cut((0, 1), 0)
    for bits in FAR_FIRST:
        forth_half(0, bits).start()
    own_copy(0).start()
    for load in loads[5:]:
        load.wait()

    @pl.loop(1, CHUNKS)
    def _(g):
        cut((0, 1, 2, 3), g)
        for bits in FAR_FIRST:
            forth(g, bits).start()
        own_copy(g).start()

    window_mask(where, bias)

    @pl.loop(0, CHUNKS)
    def _(g):
        own_copy(g).wait()

        @pl.when(g == 0)
        def _():
            for bits in range(1, 8):
                forth_half(0, bits).wait_recv()
                forth_half(1, bits).wait_recv()

        @pl.when(g > 0)
        def _():
            for bits in range(1, 8):
                forth(g, bits).wait_recv()

        attend(g, recv, res, bias, stage, held)

        @pl.when(g == CHUNKS - 1)
        def _():
            gain_start(0)

        for bits in FAR_FIRST:
            back(g, bits).start()
        own_back(g).start()

    dots[...] = jnp.zeros_like(dots)

    @pl.loop(0, CHUNKS)
    def _(g):
        @pl.when(g == 1)
        def _():
            held[1] = gain_finish(0)
            gain_start(1)

        @pl.when(g == 2)
        def _():
            held[2] = gain_finish(1)
            gain_start(2)

        @pl.when(g == CHUNKS - 1)
        def _():
            total_ref[...] = gain_finish(2)
            width = FEATURES // 64
            first = lax.axis_index("space") * width
            line = first // HDIM
            lane = first % HDIM
            back_by = (HDIM - lane) % HDIM
            place = lax.broadcasted_iota(jnp.int32, (1, HDIM), 1)
            for a in range(2):
                parts = []
                for i in (line, (line + 1) % HEADS):
                    mean = total_ref[pl.ds(a * HEADS + i, 1), :] / gain_ref[a:a + 1, lanes_of(i)]
                    parts.append(pltpu.roll(mean, back_by, 1))
                joined = jnp.where(place < HDIM - lane, parts[0], parts[1])
                gains_out_ref[a:a + 1, :] = joined[:, :width]
            for bits in range(1, 8):
                forth_half(0, bits).wait_send()
                forth_half(1, bits).wait_send()

            @pl.loop(1, CHUNKS)
            def _(i):
                for bits in range(1, 8):
                    forth(i, bits).wait_send()

            @pl.loop(0, CHUNKS - 1)
            def _(i):
                for bits in range(1, 8):
                    back(i, bits).wait_send()

        own_back(g).wait()
        for bits in range(1, 8):
            back(g, bits).wait_recv()

        @pl.loop(0, 2)
        def _(fh):
            join_block(g, fh, ret, out_ref, dv_ref, flat_x, flat_a, gain_ref, rows, scale, dots)

    for bits in range(1, 8):
        back(CHUNKS - 1, bits).wait_send()


def finish_kernel(
    out_vmem, dv_vmem, flat_x, flat_a, scale, dots, gains_vmem,
    out_ref, dq_ref, dk_ref, dv_ref, gains_ref, done, sem,
):
    whole = [
        pltpu.make_async_copy(out_vmem, out_ref, sem.at[0]),
        pltpu.make_async_copy(dv_vmem, dv_ref, sem.at[1]),
        pltpu.make_async_copy(gains_vmem, gains_ref, sem.at[2]),
    ]
    for copy in whole:
        copy.start()

    def frame(a, f):
        return pltpu.make_async_copy(done.at[a, f], (dq_ref, dk_ref)[a].at[f], sem.at[3 + 4 * a + f])

    @pl.loop(0, 4)
    def _(f):
        for a in range(2):
            r = scale[a, f]
            mean = jnp.sum(dots[a, f], axis=-1, keepdims=True) * (1.0 / FEATURES)
            factor = r * r * r * mean
            for h in range(HEADS):
                value = r * flat_a[a, f, h] - flat_x[a, f, h] * factor
                put_flat(done.at[a], f, pl.ds(h * HDIM, HDIM), value)
            frame(a, f).start()

    for copy in whole:
        copy.wait()
    for a in range(2):
        for f in range(4):
            frame(a, f).wait()


def windows(query, key, value, grad, gains):
    block = (8, CHUNKS, BLOCK, HDIM)
    natural = jax.ShapeDtypeStruct(query.shape, BF16)
    flat_rows = jax.ShapeDtypeStruct((2, 4, HEADS, PLACES, HDIM), F32)
    per_token = jax.ShapeDtypeStruct((2, 4, PLACES, HDIM), F32)
    slice_of_gains = jax.ShapeDtypeStruct((2, FEATURES // 64), F32)
    vmem = pl.BlockSpec(memory_space=pltpu.VMEM)
    hbm = pl.BlockSpec(memory_space=pltpu.HBM)
    query, key, value, grad, gains = [
        pltpu.with_memory_space_constraint(x, pltpu.HBM) for x in (query, key, value, grad, gains)
    ]
    held = pl.pallas_call(
        window_kernel,
        out_shape=(natural, natural, flat_rows, flat_rows, per_token, per_token, slice_of_gains),
        in_specs=[hbm] * 5,
        out_specs=(vmem,) * 7,
        scratch_shapes=[
            pltpu.VMEM(query.shape, BF16),
            pltpu.VMEM(query.shape, BF16),
            pltpu.VMEM(query.shape, BF16),
            pltpu.VMEM(query.shape, BF16),
            pltpu.VMEM((2, FEATURES), F32),
            pltpu.VMEM((8 * CHUNK, PLACES, HDIM), F32),
            pltpu.VMEM(block, BF16),
            pltpu.VMEM(block, BF16),
            pltpu.VMEM(block, BF16),
            pltpu.VMEM(block, BF16),
            pltpu.VMEM((TOKENS, TOKENS), F32),
            pltpu.VMEM((4, 8, CHUNK * REST, HDIM), F32),
            pltpu.VMEM((3, 2 * HEADS, HDIM), F32),
            pltpu.VMEM((17, 2 * HEADS, HDIM), F32),
            pltpu.VMEM((2 * HEADS, HDIM), F32),
            pltpu.SemaphoreType.DMA((CHUNKS + 1, 8)),
            pltpu.SemaphoreType.DMA((CHUNKS + 1, 8)),
            pltpu.SemaphoreType.DMA((CHUNKS, 8)),
            pltpu.SemaphoreType.DMA((CHUNKS, 8)),
            pltpu.SemaphoreType.DMA((2, CHUNKS)),
            pltpu.SemaphoreType.DMA((17,)),
            pltpu.SemaphoreType.DMA((17,)),
            pltpu.SemaphoreType.DMA((7,)),
        ],
        compiler_params=pltpu.CompilerParams(
            collective_id=0, has_side_effects=True, vmem_limit_bytes=32 * 1024 * 1024
        ),
        name="windows",
    )(query, key, value, grad, gains)
    return pl.pallas_call(
        finish_kernel,
        out_shape=(natural,) * 4 + (slice_of_gains,),
        in_specs=[vmem] * 7,
        out_specs=(hbm,) * 5,
        scratch_shapes=[
            pltpu.VMEM((2,) + query.shape, BF16),
            pltpu.SemaphoreType.DMA((11,)),
        ],
        compiler_params=pltpu.CompilerParams(vmem_limit_bytes=32 * 1024 * 1024),
        name="finish",
    )(*held)


def per_device(query_in, key_in, value_in, out_grad, norm_gains):
    tokens = [x[:, 0].transpose(0, 2, 1, 3) for x in (query_in, key_in, value_in, out_grad)]
    outs = windows(*tokens, norm_gains)
    return tuple(out.transpose(0, 2, 1, 3)[:, None] for out in outs[:4]) + (outs[4],)


def solution(mesh):
    token = P("tm", "space", None, None, None)
    return jax.shard_map(
        per_device,
        mesh=mesh,
        in_specs=(token, token, token, token, P()),
        out_specs=(token, token, token, token, P(None, "space")),
        check_vma=False,
    )
```

```python
import jax
import jax.numpy as jnp
from jax import lax
from jax.experimental import pallas as pl
from jax.experimental.pallas import tpu as pltpu
from jax.sharding import PartitionSpec as P

HEADS = 20
HDIM = 128
FEATURES = HEADS * HDIM
EPSILON = 1e-06
GRID_COLS = 4
GRID_ROWS = 16
TIMES = 4
CHUNK = 4
CHUNKS = HEADS // CHUNK
WIDTH = CHUNK * HDIM
COLS = 20
HALF = 10
PLACES = 2 * COLS
TOKENS = 160
MAIN = 16
REST = 4
PART = CHUNK * (MAIN + REST)
BLOCK = 4 * PART
ROOT = HDIM ** (-0.5)
MESH = pl.DeviceIdType.MESH
F32 = jnp.float32
BF16 = jnp.bfloat16
FAR_FIRST = (2, 3, 6, 7, 1, 5, 4)


def shifted(where, bits, sign):
    t, r, c = where
    t = (t + sign * (bits // 4) + TIMES) % TIMES
    r = (r + sign * (bits // 2 % 2) + GRID_ROWS) % GRID_ROWS
    c = (c + sign * (bits % 2) + GRID_COLS) % GRID_COLS
    return (t, r * GRID_COLS + c)


def gain_peers(where):
    t, r, c = where
    space = r * GRID_COLS + c
    z, xy = space % 8, space // 8
    others = [(i, j) for i in range(TIMES) for j in range(8)][1:]
    across = [((t + i) % TIMES, (xy + j) % 8 * 8 + z) for i, j in others]
    along_z = [(t, xy * 8 + (z + i) % 8) for i in range(1, 8)]
    return across, along_z


def first_row(xy):
    return xy * 5 // 2


def dot_nt(a, b):
    return lax.dot_general(a, b, (((1,), (1,)), ((), ())), preferred_element_type=F32)


def dot_nn(a, b):
    return lax.dot_general(a, b, (((1,), (0,)), ((), ())), preferred_element_type=F32)


def dot_tn(a, b):
    return lax.dot_general(a, b, (((0,), (0,)), ((), ())), preferred_element_type=F32)


def head_attention(q, k, v, g, bias):
    scores = dot_nt(q, k) * ROOT + bias
    highest = jnp.max(scores, axis=-1, keepdims=True)
    weights = jnp.exp(scores - highest)
    probs_full = weights / jnp.sum(weights, axis=-1, keepdims=True)
    probs = probs_full.astype(BF16)
    out = dot_nn(probs, v).astype(BF16)
    delta = jnp.sum(g.astype(F32) * out.astype(F32), axis=-1, keepdims=True)
    ds = (probs_full * (dot_nt(g, v) - delta) * ROOT).astype(BF16)
    dq = dot_nn(ds, k)
    dk = dot_tn(ds, q)
    dv = dot_tn(probs, g)
    return out.astype(F32), dq, dk, dv


def lanes_of(head):
    return pl.ds(pl.multiple_of(head * HDIM, HDIM), HDIM)


def flat(ref, f, lanes):
    return ref[f, :, :, lanes].reshape(PLACES, HDIM).astype(F32)


def put_flat(ref, f, lanes, value):
    ref[f, :, :, lanes] = value.astype(BF16).reshape(COLS, 2, HDIM)


def norm_scales(refs, flat_x, scale):
    @pl.loop(0, 4)
    def _(f):
        for a, ref in enumerate(refs):
            total = jnp.zeros((PLACES, HDIM), F32)
            for h in range(HEADS):
                x = flat(ref, f, pl.ds(h * HDIM, HDIM))
                flat_x[a, f, h] = x
                total = total + x * x
            mean = jnp.sum(total, axis=-1, keepdims=True) * (1.0 / FEATURES)
            scale[a, f] = jnp.broadcast_to(lax.rsqrt(mean + EPSILON), (PLACES, HDIM))


def cut_block(arrays, g, fh, flat_x, refs, gain_ref, scale, rows, sent):
    for a in arrays:
        for f in range(2):
            for h in range(CHUNK):
                head = g * CHUNK + h
                if a < 2:
                    x = flat_x[a, 2 * fh + f, head] * scale[a, 2 * fh + f]
                    x = x * gain_ref[a:a + 1, lanes_of(head)]
                else:
                    x = flat(refs[a - 2], 2 * fh + f, lanes_of(head))
                rows[(a * 2 + f) * CHUNK + h] = x
        for row in range(2):
            for ch in range(2):
                start = row + 2 * HALF * ch
                main = []
                rest = []
                for h in range(CHUNK):
                    for f in range(2):
                        i = (a * 2 + f) * CHUNK + h
                        main.append(rows[i, pl.ds(start, 8, stride=2), :])
                        rest.append(rows[i, pl.ds(start + 16, 2, stride=2), :])
                block = jnp.concatenate(main + rest, axis=0).astype(BF16)
                sent[fh * 4 + row * 2 + ch, g, a * PART:(a + 1) * PART, :] = block


def join_block(g, fh, ret, out_ref, dv_ref, flat_x, flat_a, gain_ref, rows, scale, dots):
    for a in range(4):
        for row in range(2):
            for ch in range(2):
                start = row + 2 * HALF * ch
                block = ret[fh * 4 + row * 2 + ch, g, a * PART:(a + 1) * PART, :].astype(F32)
                for h in range(CHUNK):
                    for f in range(2):
                        i = (a * 2 + f) * CHUNK + h
                        main = h * MAIN + f * 8
                        rest = CHUNK * MAIN + h * REST + f * 2
                        rows[i, pl.ds(start, 8, stride=2), :] = block[main:main + 8]
                        rows[i, pl.ds(start + 16, 2, stride=2), :] = block[rest:rest + 2]
        for f in range(2):
            frame = 2 * fh + f
            total = dots[a - 1, frame] if a in (1, 2) else None
            for h in range(CHUNK):
                head = g * CHUNK + h
                value = rows[(a * 2 + f) * CHUNK + h]
                if a in (1, 2):
                    scaled = value * gain_ref[a - 1:a, lanes_of(head)]
                    flat_a[a - 1, frame, head] = scaled
                    total = total + scaled * flat_x[a - 1, frame, head]
                else:
                    put_flat((out_ref, dv_ref)[a // 3], frame, lanes_of(head), value)
            if a in (1, 2):
                dots[a - 1, frame] = total


def window_mask(where, bias):
    owner = lax.broadcasted_iota(jnp.int32, (TOKENS, TOKENS), 0)
    other = lax.broadcasted_iota(jnp.int32, (TOKENS, TOKENS), 1)
    octants = [jnp.where(i < 8 * MAIN, i >> 4, (i - 8 * MAIN) >> 2) for i in (owner, other)]
    t, r, c = where
    edge = (
        jnp.where(t == TIMES - 1, 4, 0)
        + jnp.where(r == GRID_ROWS - 1, 2, 0)
        + jnp.where(c == GRID_COLS - 1, 1, 0)
    )
    bias[...] = jnp.where(((octants[0] ^ octants[1]) & edge) == 0, 0.0, -1e30)


def attend(g, recv, res, bias, stage, sums):
    ends = [
        [
            recv[bits, g, a * PART + CHUNK * MAIN:(a + 1) * PART, :].astype(F32)
            for bits in range(8)
        ]
        for a in range(4)
    ]
    for h in range(CHUNK):
        window = []
        for a in range(4):
            start = a * PART + h * MAIN
            mains = [recv[bits, g, start:start + MAIN, :] for bits in range(8)]
            rests = [ends[a][bits][h * REST:(h + 1) * REST] for bits in range(8)]
            window.append(jnp.concatenate(mains + [jnp.concatenate(rests, axis=0).astype(BF16)], axis=0))
        results = head_attention(*window, bias[...])
        for a in range(4):
            start = a * PART + h * MAIN
            for bits in range(8):
                res[bits, g, start:start + MAIN, :] = results[a][bits * MAIN:(bits + 1) * MAIN].astype(BF16)
                rest = 8 * MAIN + bits * REST
                stage[a, bits, h * REST:(h + 1) * REST, :] = results[a][rest:rest + REST]
        for a in range(2):
            terms = results[1 + a].astype(BF16).astype(F32) * window[a].astype(F32)
            sums[g * CHUNK + h, a:a + 1, :] = jnp.sum(terms, axis=0, keepdims=True)
    for bits in range(8):
        for a in range(4):
            res[bits, g, a * PART + CHUNK * MAIN:(a + 1) * PART, :] = stage[a, bits].astype(BF16)


def window_kernel(
    q_hbm, k_hbm, v_hbm, g_hbm, gain_hbm,
    out_ref, dv_ref, flat_x, flat_a, scale, dots, gains_out_ref,
    q_ref, k_ref, v_ref, g_ref, gain_ref,
    rows, sent, recv, res, ret, bias, stage, sums, partial, slots,
    fsend, frecv, bsend, brecv, own_sem, gsend, grecv, in_sem,
):
    where = (
        lax.axis_index("tm"),
        lax.axis_index("space") // GRID_COLS,
        lax.axis_index("space") % GRID_COLS,
    )
    early = pl.ds(0, WIDTH)
    late = pl.ds(WIDTH, FEATURES - WIDTH)
    loads = [
        pltpu.make_async_copy(v_hbm.at[:, :, :, early], v_ref.at[:, :, :, early], in_sem.at[0]),
        pltpu.make_async_copy(g_hbm.at[:, :, :, early], g_ref.at[:, :, :, early], in_sem.at[1]),
        pltpu.make_async_copy(q_hbm, q_ref, in_sem.at[2]),
        pltpu.make_async_copy(k_hbm, k_ref, in_sem.at[3]),
        pltpu.make_async_copy(gain_hbm, gain_ref, in_sem.at[4]),
        pltpu.make_async_copy(v_hbm.at[:, :, :, late], v_ref.at[:, :, :, late], in_sem.at[5]),
        pltpu.make_async_copy(g_hbm.at[:, :, :, late], g_ref.at[:, :, :, late], in_sem.at[6]),
    ]
    for load in loads:
        load.start()

    rounds = gain_peers(where)
    barrier = pltpu.get_barrier_semaphore()
    for bits in range(1, 8):
        for sign in (-1, 1):
            pl.semaphore_signal(barrier, inc=1, device_id=shifted(where, bits, sign), device_id_type=MESH)
    for group in rounds:
        for device in group:
            pl.semaphore_signal(barrier, inc=1, device_id=device, device_id_type=MESH)

    def own_copy(g):
        return pltpu.make_async_copy(sent.at[7, g], recv.at[0, g], own_sem.at[0, g])

    def own_back(g):
        return pltpu.make_async_copy(res.at[0, g], ret.at[7, g], own_sem.at[1, g])

    def forth(g, bits):
        return pltpu.make_async_remote_copy(
            src_ref=sent.at[7 - bits, g],
            dst_ref=recv.at[bits, g],
            send_sem=fsend.at[g, bits],
            recv_sem=frecv.at[g, bits],
            device_id=shifted(where, bits, -1),
            device_id_type=MESH,
        )

    def forth_half(half, bits):
        part = pl.ds(half * 2 * PART, 2 * PART)
        sem = (CHUNKS, 0)[half]
        return pltpu.make_async_remote_copy(
            src_ref=sent.at[7 - bits, 0, part],
            dst_ref=recv.at[bits, 0, part],
            send_sem=fsend.at[sem, bits],
            recv_sem=frecv.at[sem, bits],
            device_id=shifted(where, bits, -1),
            device_id_type=MESH,
        )

    def back(g, bits):
        return pltpu.make_async_remote_copy(
            src_ref=res.at[bits, g],
            dst_ref=ret.at[7 - bits, g],
            send_sem=bsend.at[g, bits],
            recv_sem=brecv.at[g, bits],
            device_id=shifted(where, bits, 1),
            device_id_type=MESH,
        )

    def gain_copies(step):
        base = (0, 31)[step]
        copies = []
        for i, device in enumerate(rounds[step]):
            if step == 0:
                source = sums.at[pl.ds(first_row(device[1] // 8), 3)]
            else:
                source = partial.at[step - 1]
            copies.append(
                pltpu.make_async_remote_copy(
                    src_ref=source,
                    dst_ref=slots.at[base + i],
                    send_sem=gsend.at[base + i],
                    recv_sem=grecv.at[base + i],
                    device_id=device,
                    device_id_type=MESH,
                )
            )
        return copies

    def gain_start(step):
        for copy in gain_copies(step):
            copy.start()

    def gain_finish(step):
        base = (0, 31)[step]
        if step == 0:
            total = sums[pl.ds(first_row(lax.axis_index("space") // 8), 3)]
        else:
            total = partial[step - 1]
        for i, copy in enumerate(gain_copies(step)):
            copy.wait()
            total = total + slots[base + i]
        partial[step] = total

    def cut(arrays, g):
        @pl.loop(0, 2)
        def _(fh):
            cut_block(arrays, g, fh, flat_x, (v_ref, g_ref), gain_ref, scale, rows, sent)

    loads[0].wait()
    loads[1].wait()
    cut((2, 3), 0)
    pl.semaphore_wait(barrier, 14 + 31 + 7)
    for bits in FAR_FIRST:
        forth_half(1, bits).start()
    for load in loads[2:5]:
        load.wait()
    norm_scales((q_ref, k_ref), flat_x, scale)
    cut((0, 1), 0)
    for bits in FAR_FIRST:
        forth_half(0, bits).start()
    own_copy(0).start()
    for load in loads[5:]:
        load.wait()

    @pl.loop(1, CHUNKS)
    def _(g):
        cut((0, 1, 2, 3), g)
        for bits in FAR_FIRST:
            forth(g, bits).start()
        own_copy(g).start()

    window_mask(where, bias)

    @pl.loop(0, CHUNKS)
    def _(g):
        own_copy(g).wait()

        @pl.when(g == 0)
        def _():
            for bits in range(1, 8):
                forth_half(0, bits).wait_recv()
                forth_half(1, bits).wait_recv()

        @pl.when(g > 0)
        def _():
            for bits in range(1, 8):
                forth(g, bits).wait_recv()

        attend(g, recv, res, bias, stage, sums)

        @pl.when(g == CHUNKS - 1)
        def _():
            gain_start(0)

        for bits in FAR_FIRST:
            back(g, bits).start()
        own_back(g).start()

    dots[...] = jnp.zeros_like(dots)

    @pl.loop(0, CHUNKS)
    def _(g):
        @pl.when(g == 1)
        def _():
            gain_finish(0)
            gain_start(1)

        @pl.when(g == CHUNKS - 1)
        def _():
            gain_finish(1)
            width = FEATURES // 64
            first = lax.axis_index("space") * width
            row = first_row(lax.axis_index("space") // 8)
            line = first // HDIM - row
            lane = first % HDIM
            back_by = (HDIM - lane) % HDIM
            place = lax.broadcasted_iota(jnp.int32, (1, HDIM), 1)
            for a in range(2):
                parts = []
                for i in (line, (line + 1) % 3):
                    mean = partial[1, i, a:a + 1, :] / gain_ref[a:a + 1, lanes_of(row + i)]
                    parts.append(pltpu.roll(mean, back_by, 1))
                joined = jnp.where(place < HDIM - lane, parts[0], parts[1])
                gains_out_ref[a:a + 1, :] = joined[:, :width]
            for bits in range(1, 8):
                forth_half(0, bits).wait_send()
                forth_half(1, bits).wait_send()

            @pl.loop(1, CHUNKS)
            def _(i):
                for bits in range(1, 8):
                    forth(i, bits).wait_send()

            @pl.loop(0, CHUNKS - 1)
            def _(i):
                for bits in range(1, 8):
                    back(i, bits).wait_send()

        own_back(g).wait()
        for bits in range(1, 8):
            back(g, bits).wait_recv()

        @pl.loop(0, 2)
        def _(fh):
            join_block(g, fh, ret, out_ref, dv_ref, flat_x, flat_a, gain_ref, rows, scale, dots)

    for bits in range(1, 8):
        back(CHUNKS - 1, bits).wait_send()


def finish_kernel(
    out_vmem, dv_vmem, flat_x, flat_a, scale, dots, gains_vmem,
    out_ref, dq_ref, dk_ref, dv_ref, gains_ref, done, sem,
):
    whole = [
        pltpu.make_async_copy(out_vmem, out_ref, sem.at[0]),
        pltpu.make_async_copy(dv_vmem, dv_ref, sem.at[1]),
        pltpu.make_async_copy(gains_vmem, gains_ref, sem.at[2]),
    ]
    for copy in whole:
        copy.start()

    def frame(a, f):
        return pltpu.make_async_copy(done.at[a, f], (dq_ref, dk_ref)[a].at[f], sem.at[3 + 4 * a + f])

    @pl.loop(0, 4)
    def _(f):
        for a in range(2):
            r = scale[a, f]
            mean = jnp.sum(dots[a, f], axis=-1, keepdims=True) * (1.0 / FEATURES)
            factor = r * r * r * mean
            for h in range(HEADS):
                value = r * flat_a[a, f, h] - flat_x[a, f, h] * factor
                put_flat(done.at[a], f, pl.ds(h * HDIM, HDIM), value)
            frame(a, f).start()

    for copy in whole:
        copy.wait()
    for a in range(2):
        for f in range(4):
            frame(a, f).wait()


def windows(query, key, value, grad, gains):
    block = (8, CHUNKS, BLOCK, HDIM)
    natural = jax.ShapeDtypeStruct(query.shape, BF16)
    flat_rows = jax.ShapeDtypeStruct((2, 4, HEADS, PLACES, HDIM), F32)
    per_token = jax.ShapeDtypeStruct((2, 4, PLACES, HDIM), F32)
    slice_of_gains = jax.ShapeDtypeStruct((2, FEATURES // 64), F32)
    vmem = pl.BlockSpec(memory_space=pltpu.VMEM)
    hbm = pl.BlockSpec(memory_space=pltpu.HBM)
    query, key, value, grad, gains = [
        pltpu.with_memory_space_constraint(x, pltpu.HBM) for x in (query, key, value, grad, gains)
    ]
    held = pl.pallas_call(
        window_kernel,
        out_shape=(natural, natural, flat_rows, flat_rows, per_token, per_token, slice_of_gains),
        in_specs=[hbm] * 5,
        out_specs=(vmem,) * 7,
        scratch_shapes=[
            pltpu.VMEM(query.shape, BF16),
            pltpu.VMEM(query.shape, BF16),
            pltpu.VMEM(query.shape, BF16),
            pltpu.VMEM(query.shape, BF16),
            pltpu.VMEM((2, FEATURES), F32),
            pltpu.VMEM((8 * CHUNK, PLACES, HDIM), F32),
            pltpu.VMEM(block, BF16),
            pltpu.VMEM(block, BF16),
            pltpu.VMEM(block, BF16),
            pltpu.VMEM(block, BF16),
            pltpu.VMEM((TOKENS, TOKENS), F32),
            pltpu.VMEM((4, 8, CHUNK * REST, HDIM), F32),
            pltpu.VMEM((HEADS, 2, HDIM), F32),
            pltpu.VMEM((2, 3, 2, HDIM), F32),
            pltpu.VMEM((38, 3, 2, HDIM), F32),
            pltpu.SemaphoreType.DMA((CHUNKS + 1, 8)),
            pltpu.SemaphoreType.DMA((CHUNKS + 1, 8)),
            pltpu.SemaphoreType.DMA((CHUNKS, 8)),
            pltpu.SemaphoreType.DMA((CHUNKS, 8)),
            pltpu.SemaphoreType.DMA((2, CHUNKS)),
            pltpu.SemaphoreType.DMA((38,)),
            pltpu.SemaphoreType.DMA((38,)),
            pltpu.SemaphoreType.DMA((7,)),
        ],
        compiler_params=pltpu.CompilerParams(
            collective_id=0, has_side_effects=True, vmem_limit_bytes=32 * 1024 * 1024
        ),
        name="windows",
    )(query, key, value, grad, gains)
    return pl.pallas_call(
        finish_kernel,
        out_shape=(natural,) * 4 + (slice_of_gains,),
        in_specs=[vmem] * 7,
        out_specs=(hbm,) * 5,
        scratch_shapes=[
            pltpu.VMEM((2,) + query.shape, BF16),
            pltpu.SemaphoreType.DMA((11,)),
        ],
        compiler_params=pltpu.CompilerParams(vmem_limit_bytes=32 * 1024 * 1024),
        name="finish",
    )(*held)


def per_device(query_in, key_in, value_in, out_grad, norm_gains):
    tokens = [x[:, 0].transpose(0, 2, 1, 3) for x in (query_in, key_in, value_in, out_grad)]
    outs = windows(*tokens, norm_gains)
    return tuple(out.transpose(0, 2, 1, 3)[:, None] for out in outs[:4]) + (outs[4],)


def solution(mesh):
    token = P("tm", "space", None, None, None)
    return jax.shard_map(
        per_device,
        mesh=mesh,
        in_specs=(token, token, token, token, P()),
        out_specs=(token, token, token, token, P(None, "space")),
        check_vma=False,
    )
```

```python
import jax
import jax.numpy as jnp
from jax import lax
from jax.experimental import pallas as pl
from jax.experimental.pallas import tpu as pltpu
from jax.sharding import PartitionSpec as P

HEADS = 20
HDIM = 128
FEATURES = HEADS * HDIM
EPSILON = 1e-06
GRID_COLS = 4
GRID_ROWS = 16
TIMES = 4
CHUNK = 4
CHUNKS = HEADS // CHUNK
WIDTH = CHUNK * HDIM
COLS = 20
HALF = 10
PLACES = 2 * COLS
TOKENS = 160
MAIN = 16
REST = 4
PART = CHUNK * (MAIN + REST)
BLOCK = 4 * PART
ROOT = HDIM ** (-0.5)
MESH = pl.DeviceIdType.MESH
F32 = jnp.float32
BF16 = jnp.bfloat16
FAR_FIRST = (2, 3, 6, 7, 1, 5, 4)
BACK_ORDER = (2, 3, 1, 6, 7, 5, 4)


def shifted(where, bits, sign):
    t, r, c = where
    t = (t + sign * (bits // 4) + TIMES) % TIMES
    r = (r + sign * (bits // 2 % 2) + GRID_ROWS) % GRID_ROWS
    c = (c + sign * (bits % 2) + GRID_COLS) % GRID_COLS
    return (t, r * GRID_COLS + c)


def gain_peers(where):
    t, r, c = where
    space = r * GRID_COLS + c
    z, xy = space % 8, space // 8
    others = [(i, j) for i in range(TIMES) for j in range(8)][1:]
    across = [((t + i) % TIMES, (xy + j) % 8 * 8 + z) for i, j in others]
    along_z = [(t, xy * 8 + (z + i) % 8) for i in range(1, 8)]
    return across, along_z


def first_row(xy):
    return xy * 5 // 2


def dot_nt(a, b):
    return lax.dot_general(a, b, (((1,), (1,)), ((), ())), preferred_element_type=F32)


def dot_nn(a, b):
    return lax.dot_general(a, b, (((1,), (0,)), ((), ())), preferred_element_type=F32)


def dot_tn(a, b):
    return lax.dot_general(a, b, (((0,), (0,)), ((), ())), preferred_element_type=F32)


def head_attention(q, k, v, g, bias):
    scores = dot_nt(q, k) * ROOT + bias
    highest = jnp.max(scores, axis=-1, keepdims=True)
    weights = jnp.exp(scores - highest)
    probs_full = weights / jnp.sum(weights, axis=-1, keepdims=True)
    probs = probs_full.astype(BF16)
    out = dot_nn(probs, v).astype(BF16)
    delta = jnp.sum(g.astype(F32) * out.astype(F32), axis=-1, keepdims=True)
    ds = (probs_full * (dot_nt(g, v) - delta) * ROOT).astype(BF16)
    dq = dot_nn(ds, k)
    dk = dot_tn(ds, q)
    dv = dot_tn(probs, g)
    return out.astype(F32), dq, dk, dv


def lanes_of(head):
    return pl.ds(pl.multiple_of(head * HDIM, HDIM), HDIM)


def flat(ref, f, lanes):
    return ref[f, :, :, lanes].reshape(PLACES, HDIM).astype(F32)


def put_flat(ref, f, lanes, value):
    ref[f, :, :, lanes] = value.astype(BF16).reshape(COLS, 2, HDIM)


def norm_scales(refs, flat_x, scale):
    @pl.loop(0, 4)
    def _(f):
        for a, ref in enumerate(refs):
            total = jnp.zeros((PLACES, HDIM), F32)
            for h in range(HEADS):
                x = flat(ref, f, pl.ds(h * HDIM, HDIM))
                flat_x[a, f, h] = x
                total = total + x * x
            mean = jnp.sum(total, axis=-1, keepdims=True) * (1.0 / FEATURES)
            scale[a, f] = jnp.broadcast_to(lax.rsqrt(mean + EPSILON), (PLACES, HDIM))


def cut_block(arrays, g, fh, flat_x, refs, gain_ref, scale, rows, sent):
    for a in arrays:
        for f in range(2):
            for h in range(CHUNK):
                head = g * CHUNK + h
                if a < 2:
                    x = flat_x[a, 2 * fh + f, head] * scale[a, 2 * fh + f]
                    x = x * gain_ref[a:a + 1, lanes_of(head)]
                else:
                    x = flat(refs[a - 2], 2 * fh + f, lanes_of(head))
                rows[(a * 2 + f) * CHUNK + h] = x
        for row in range(2):
            for ch in range(2):
                start = row + 2 * HALF * ch
                main = []
                rest = []
                for h in range(CHUNK):
                    for f in range(2):
                        i = (a * 2 + f) * CHUNK + h
                        main.append(rows[i, pl.ds(start, 8, stride=2), :])
                        rest.append(rows[i, pl.ds(start + 16, 2, stride=2), :])
                block = jnp.concatenate(main + rest, axis=0).astype(BF16)
                sent[fh * 4 + row * 2 + ch, g, a * PART:(a + 1) * PART, :] = block


def join_block(g, fh, ret, out_ref, dv_ref, flat_x, flat_a, gain_ref, rows, scale, dots):
    for a in range(4):
        for row in range(2):
            for ch in range(2):
                start = row + 2 * HALF * ch
                block = ret[fh * 4 + row * 2 + ch, g, a * PART:(a + 1) * PART, :].astype(F32)
                for h in range(CHUNK):
                    for f in range(2):
                        i = (a * 2 + f) * CHUNK + h
                        main = h * MAIN + f * 8
                        rest = CHUNK * MAIN + h * REST + f * 2
                        rows[i, pl.ds(start, 8, stride=2), :] = block[main:main + 8]
                        rows[i, pl.ds(start + 16, 2, stride=2), :] = block[rest:rest + 2]
        for f in range(2):
            frame = 2 * fh + f
            total = dots[a - 1, frame] if a in (1, 2) else None
            for h in range(CHUNK):
                head = g * CHUNK + h
                value = rows[(a * 2 + f) * CHUNK + h]
                if a in (1, 2):
                    scaled = value * gain_ref[a - 1:a, lanes_of(head)]
                    flat_a[a - 1, frame, head] = scaled
                    total = total + scaled * flat_x[a - 1, frame, head]
                else:
                    put_flat((out_ref, dv_ref)[a // 3], frame, lanes_of(head), value)
            if a in (1, 2):
                dots[a - 1, frame] = total


def window_mask(where, bias):
    owner = lax.broadcasted_iota(jnp.int32, (TOKENS, TOKENS), 0)
    other = lax.broadcasted_iota(jnp.int32, (TOKENS, TOKENS), 1)
    octants = [jnp.where(i < 8 * MAIN, i >> 4, (i - 8 * MAIN) >> 2) for i in (owner, other)]
    t, r, c = where
    edge = (
        jnp.where(t == TIMES - 1, 4, 0)
        + jnp.where(r == GRID_ROWS - 1, 2, 0)
        + jnp.where(c == GRID_COLS - 1, 1, 0)
    )
    bias[...] = jnp.where(((octants[0] ^ octants[1]) & edge) == 0, 0.0, -1e30)


def attend(g, recv, res, bias, stage, sums):
    ends = [
        [
            recv[bits, g, a * PART + CHUNK * MAIN:(a + 1) * PART, :].astype(F32)
            for bits in range(8)
        ]
        for a in range(4)
    ]
    for h in range(CHUNK):
        window = []
        for a in range(4):
            start = a * PART + h * MAIN
            mains = [recv[bits, g, start:start + MAIN, :] for bits in range(8)]
            rests = [ends[a][bits][h * REST:(h + 1) * REST] for bits in range(8)]
            window.append(jnp.concatenate(mains + [jnp.concatenate(rests, axis=0).astype(BF16)], axis=0))
        results = head_attention(*window, bias[...])
        for a in range(4):
            start = a * PART + h * MAIN
            for bits in range(8):
                res[bits, g, start:start + MAIN, :] = results[a][bits * MAIN:(bits + 1) * MAIN].astype(BF16)
                rest = 8 * MAIN + bits * REST
                stage[a, bits, h * REST:(h + 1) * REST, :] = results[a][rest:rest + REST]
        for a in range(2):
            terms = results[1 + a].astype(BF16).astype(F32) * window[a].astype(F32)
            sums[g * CHUNK + h, a:a + 1, :] = jnp.sum(terms, axis=0, keepdims=True)
    for bits in range(8):
        for a in range(4):
            res[bits, g, a * PART + CHUNK * MAIN:(a + 1) * PART, :] = stage[a, bits].astype(BF16)


def window_kernel(
    q_hbm, k_hbm, v_hbm, g_hbm, gain_hbm,
    out_ref, dv_ref, flat_x, flat_a, scale, dots, gains_out_ref,
    q_ref, k_ref, v_ref, g_ref, gain_ref,
    rows, sent, recv, res, ret, bias, stage, sums, partial, slots,
    fsend, frecv, bsend, brecv, own_sem, gsend, grecv, in_sem,
):
    where = (
        lax.axis_index("tm"),
        lax.axis_index("space") // GRID_COLS,
        lax.axis_index("space") % GRID_COLS,
    )
    early = pl.ds(0, WIDTH)
    late = pl.ds(WIDTH, FEATURES - WIDTH)
    loads = [
        pltpu.make_async_copy(v_hbm.at[:, :, :, early], v_ref.at[:, :, :, early], in_sem.at[0]),
        pltpu.make_async_copy(g_hbm.at[:, :, :, early], g_ref.at[:, :, :, early], in_sem.at[1]),
        pltpu.make_async_copy(q_hbm, q_ref, in_sem.at[2]),
        pltpu.make_async_copy(k_hbm, k_ref, in_sem.at[3]),
        pltpu.make_async_copy(gain_hbm, gain_ref, in_sem.at[4]),
        pltpu.make_async_copy(v_hbm.at[:, :, :, late], v_ref.at[:, :, :, late], in_sem.at[5]),
        pltpu.make_async_copy(g_hbm.at[:, :, :, late], g_ref.at[:, :, :, late], in_sem.at[6]),
    ]
    for load in loads[:2]:
        load.start()

    rounds = gain_peers(where)
    barrier = pltpu.get_barrier_semaphore()
    for bits in range(1, 8):
        for sign in (-1, 1):
            pl.semaphore_signal(barrier, inc=1, device_id=shifted(where, bits, sign), device_id_type=MESH)
    for group in rounds:
        for device in group:
            pl.semaphore_signal(barrier, inc=1, device_id=device, device_id_type=MESH)

    for load in loads[2:]:
        load.start()

    def own_copy(g):
        return pltpu.make_async_copy(sent.at[7, g], recv.at[0, g], own_sem.at[0, g])

    def own_back(g):
        return pltpu.make_async_copy(res.at[0, g], ret.at[7, g], own_sem.at[1, g])

    def forth(g, bits):
        return pltpu.make_async_remote_copy(
            src_ref=sent.at[7 - bits, g],
            dst_ref=recv.at[bits, g],
            send_sem=fsend.at[g, bits],
            recv_sem=frecv.at[g, bits],
            device_id=shifted(where, bits, -1),
            device_id_type=MESH,
        )

    def forth_half(half, bits):
        part = pl.ds(half * 2 * PART, 2 * PART)
        sem = (CHUNKS, 0)[half]
        return pltpu.make_async_remote_copy(
            src_ref=sent.at[7 - bits, 0, part],
            dst_ref=recv.at[bits, 0, part],
            send_sem=fsend.at[sem, bits],
            recv_sem=frecv.at[sem, bits],
            device_id=shifted(where, bits, -1),
            device_id_type=MESH,
        )

    def back(g, bits):
        return pltpu.make_async_remote_copy(
            src_ref=res.at[bits, g],
            dst_ref=ret.at[7 - bits, g],
            send_sem=bsend.at[g, bits],
            recv_sem=brecv.at[g, bits],
            device_id=shifted(where, bits, 1),
            device_id_type=MESH,
        )

    def gain_copies(step):
        base = (0, 31)[step]
        copies = []
        for i, device in enumerate(rounds[step]):
            if step == 0:
                source = sums.at[pl.ds(first_row(device[1] // 8), 3)]
            else:
                source = partial.at[step - 1]
            copies.append(
                pltpu.make_async_remote_copy(
                    src_ref=source,
                    dst_ref=slots.at[base + i],
                    send_sem=gsend.at[base + i],
                    recv_sem=grecv.at[base + i],
                    device_id=device,
                    device_id_type=MESH,
                )
            )
        return copies

    def gain_start(step):
        for copy in gain_copies(step):
            copy.start()

    def gain_finish(step):
        base = (0, 31)[step]
        if step == 0:
            total = sums[pl.ds(first_row(lax.axis_index("space") // 8), 3)]
        else:
            total = partial[step - 1]
        for i, copy in enumerate(gain_copies(step)):
            copy.wait()
            total = total + slots[base + i]
        partial[step] = total

    def cut(arrays, g):
        @pl.loop(0, 2)
        def _(fh):
            cut_block(arrays, g, fh, flat_x, (v_ref, g_ref), gain_ref, scale, rows, sent)

    loads[0].wait()
    loads[1].wait()
    cut((2, 3), 0)
    pl.semaphore_wait(barrier, 14 + 31 + 7)
    for bits in FAR_FIRST:
        forth_half(1, bits).start()
    for load in loads[2:5]:
        load.wait()
    norm_scales((q_ref, k_ref), flat_x, scale)
    cut((0, 1), 0)
    for bits in FAR_FIRST:
        forth_half(0, bits).start()
    own_copy(0).start()
    for load in loads[5:]:
        load.wait()

    @pl.loop(1, CHUNKS)
    def _(g):
        cut((0, 1, 2, 3), g)
        for bits in FAR_FIRST:
            forth(g, bits).start()
        own_copy(g).start()

    window_mask(where, bias)

    @pl.loop(0, CHUNKS)
    def _(g):
        own_copy(g).wait()

        @pl.when(g == 0)
        def _():
            for bits in range(1, 8):
                forth_half(0, bits).wait_recv()
                forth_half(1, bits).wait_recv()

        @pl.when(g > 0)
        def _():
            for bits in range(1, 8):
                forth(g, bits).wait_recv()

        attend(g, recv, res, bias, stage, sums)

        for bits in BACK_ORDER:
            back(g, bits).start()
        own_back(g).start()

        @pl.when(g == CHUNKS - 1)
        def _():
            gain_start(0)

    dots[...] = jnp.zeros_like(dots)

    @pl.loop(0, CHUNKS)
    def _(g):
        @pl.when(g == 1)
        def _():
            gain_finish(0)
            gain_start(1)

        @pl.when(g == CHUNKS - 1)
        def _():
            gain_finish(1)
            width = FEATURES // 64
            first = lax.axis_index("space") * width
            row = first_row(lax.axis_index("space") // 8)
            line = first // HDIM - row
            lane = first % HDIM
            back_by = (HDIM - lane) % HDIM
            place = lax.broadcasted_iota(jnp.int32, (1, HDIM), 1)
            for a in range(2):
                parts = []
                for i in (line, (line + 1) % 3):
                    mean = partial[1, i, a:a + 1, :] / gain_ref[a:a + 1, lanes_of(row + i)]
                    parts.append(pltpu.roll(mean, back_by, 1))
                joined = jnp.where(place < HDIM - lane, parts[0], parts[1])
                gains_out_ref[a:a + 1, :] = joined[:, :width]
            for bits in range(1, 8):
                forth_half(0, bits).wait_send()
                forth_half(1, bits).wait_send()

            @pl.loop(1, CHUNKS)
            def _(i):
                for bits in range(1, 8):
                    forth(i, bits).wait_send()

            @pl.loop(0, CHUNKS - 1)
            def _(i):
                for bits in range(1, 8):
                    back(i, bits).wait_send()

        own_back(g).wait()
        for fh, group in ((1, (1, 2, 3)), (0, (4, 5, 6, 7))):
            for bits in group:
                back(g, bits).wait_recv()
            join_block(g, fh, ret, out_ref, dv_ref, flat_x, flat_a, gain_ref, rows, scale, dots)

    for bits in range(1, 8):
        back(CHUNKS - 1, bits).wait_send()


def finish_kernel(
    out_vmem, dv_vmem, flat_x, flat_a, scale, dots, gains_vmem,
    out_ref, dq_ref, dk_ref, dv_ref, gains_ref, done, sem,
):
    whole = [
        pltpu.make_async_copy(out_vmem, out_ref, sem.at[0]),
        pltpu.make_async_copy(dv_vmem, dv_ref, sem.at[1]),
        pltpu.make_async_copy(gains_vmem, gains_ref, sem.at[2]),
    ]
    for copy in whole:
        copy.start()

    def frame(a, f):
        return pltpu.make_async_copy(done.at[a, f], (dq_ref, dk_ref)[a].at[f], sem.at[3 + 4 * a + f])

    @pl.loop(0, 4)
    def _(f):
        for a in range(2):
            r = scale[a, f]
            mean = jnp.sum(dots[a, f], axis=-1, keepdims=True) * (1.0 / FEATURES)
            factor = r * r * r * mean
            for h in range(HEADS):
                value = r * flat_a[a, f, h] - flat_x[a, f, h] * factor
                put_flat(done.at[a], f, pl.ds(h * HDIM, HDIM), value)
            frame(a, f).start()

    for copy in whole:
        copy.wait()
    for a in range(2):
        for f in range(4):
            frame(a, f).wait()


def windows(query, key, value, grad, gains):
    block = (8, CHUNKS, BLOCK, HDIM)
    natural = jax.ShapeDtypeStruct(query.shape, BF16)
    flat_rows = jax.ShapeDtypeStruct((2, 4, HEADS, PLACES, HDIM), F32)
    per_token = jax.ShapeDtypeStruct((2, 4, PLACES, HDIM), F32)
    slice_of_gains = jax.ShapeDtypeStruct((2, FEATURES // 64), F32)
    vmem = pl.BlockSpec(memory_space=pltpu.VMEM)
    hbm = pl.BlockSpec(memory_space=pltpu.HBM)
    query, key, value, grad, gains = [
        pltpu.with_memory_space_constraint(x, pltpu.HBM) for x in (query, key, value, grad, gains)
    ]
    held = pl.pallas_call(
        window_kernel,
        out_shape=(natural, natural, flat_rows, flat_rows, per_token, per_token, slice_of_gains),
        in_specs=[hbm] * 5,
        out_specs=(vmem,) * 7,
        scratch_shapes=[
            pltpu.VMEM(query.shape, BF16),
            pltpu.VMEM(query.shape, BF16),
            pltpu.VMEM(query.shape, BF16),
            pltpu.VMEM(query.shape, BF16),
            pltpu.VMEM((2, FEATURES), F32),
            pltpu.VMEM((8 * CHUNK, PLACES, HDIM), F32),
            pltpu.VMEM(block, BF16),
            pltpu.VMEM(block, BF16),
            pltpu.VMEM(block, BF16),
            pltpu.VMEM(block, BF16),
            pltpu.VMEM((TOKENS, TOKENS), F32),
            pltpu.VMEM((4, 8, CHUNK * REST, HDIM), F32),
            pltpu.VMEM((HEADS, 2, HDIM), F32),
            pltpu.VMEM((2, 3, 2, HDIM), F32),
            pltpu.VMEM((38, 3, 2, HDIM), F32),
            pltpu.SemaphoreType.DMA((CHUNKS + 1, 8)),
            pltpu.SemaphoreType.DMA((CHUNKS + 1, 8)),
            pltpu.SemaphoreType.DMA((CHUNKS, 8)),
            pltpu.SemaphoreType.DMA((CHUNKS, 8)),
            pltpu.SemaphoreType.DMA((2, CHUNKS)),
            pltpu.SemaphoreType.DMA((38,)),
            pltpu.SemaphoreType.DMA((38,)),
            pltpu.SemaphoreType.DMA((7,)),
        ],
        compiler_params=pltpu.CompilerParams(
            collective_id=0, has_side_effects=True, vmem_limit_bytes=32 * 1024 * 1024
        ),
        name="windows",
    )(query, key, value, grad, gains)
    return pl.pallas_call(
        finish_kernel,
        out_shape=(natural,) * 4 + (slice_of_gains,),
        in_specs=[vmem] * 7,
        out_specs=(hbm,) * 5,
        scratch_shapes=[
            pltpu.VMEM((2,) + query.shape, BF16),
            pltpu.SemaphoreType.DMA((11,)),
        ],
        compiler_params=pltpu.CompilerParams(vmem_limit_bytes=32 * 1024 * 1024),
        name="finish",
    )(*held)


def per_device(query_in, key_in, value_in, out_grad, norm_gains):
    tokens = [x[:, 0].transpose(0, 2, 1, 3) for x in (query_in, key_in, value_in, out_grad)]
    outs = windows(*tokens, norm_gains)
    return tuple(out.transpose(0, 2, 1, 3)[:, None] for out in outs[:4]) + (outs[4],)


def solution(mesh):
    token = P("tm", "space", None, None, None)
    return jax.shard_map(
        per_device,
        mesh=mesh,
        in_specs=(token, token, token, token, P()),
        out_specs=(token, token, token, token, P(None, "space")),
        check_vma=False,
    )
```

```python
import jax
import jax.numpy as jnp
from jax import lax
from jax.experimental import pallas as pl
from jax.experimental.pallas import tpu as pltpu
from jax.sharding import PartitionSpec as P

HEADS = 20
HDIM = 128
FEATURES = HEADS * HDIM
EPSILON = 1e-06
GRID_COLS = 4
GRID_ROWS = 16
TIMES = 4
CHUNK = 4
CHUNKS = HEADS // CHUNK
WIDTH = CHUNK * HDIM
COLS = 20
HALF = 10
PLACES = 2 * COLS
TOKENS = 160
MAIN = 16
REST = 4
PART = CHUNK * (MAIN + REST)
BLOCK = 4 * PART
ROOT = HDIM ** (-0.5)
MESH = pl.DeviceIdType.MESH
F32 = jnp.float32
BF16 = jnp.bfloat16
FAR_FIRST = (2, 3, 6, 7, 1, 5, 4)


def shifted(where, bits, sign):
    t, r, c = where
    t = (t + sign * (bits // 4) + TIMES) % TIMES
    r = (r + sign * (bits // 2 % 2) + GRID_ROWS) % GRID_ROWS
    c = (c + sign * (bits % 2) + GRID_COLS) % GRID_COLS
    return (t, r * GRID_COLS + c)


def gain_peers(where):
    t, r, c = where
    space = r * GRID_COLS + c
    z, xy = space % 8, space // 8
    others = [(i, j) for i in range(TIMES) for j in range(8)][1:]
    across = [((t + i) % TIMES, (xy + j) % 8 * 8 + z) for i, j in others]
    along_z = [(t, xy * 8 + (z + i) % 8) for i in range(1, 8)]
    return across, along_z


def first_row(xy):
    return xy * 5 // 2


def dot_nt(a, b):
    return lax.dot_general(a, b, (((1,), (1,)), ((), ())), preferred_element_type=F32)


def dot_nn(a, b):
    return lax.dot_general(a, b, (((1,), (0,)), ((), ())), preferred_element_type=F32)


def dot_tn(a, b):
    return lax.dot_general(a, b, (((0,), (0,)), ((), ())), preferred_element_type=F32)


def head_attention(q, k, v, g, bias):
    scores = dot_nt(q, k) * ROOT + bias
    highest = jnp.max(scores, axis=-1, keepdims=True)
    weights = jnp.exp(scores - highest)
    probs_full = weights / jnp.sum(weights, axis=-1, keepdims=True)
    probs = probs_full.astype(BF16)
    out = dot_nn(probs, v).astype(BF16)
    delta = jnp.sum(g.astype(F32) * out.astype(F32), axis=-1, keepdims=True)
    ds = (probs_full * (dot_nt(g, v) - delta) * ROOT).astype(BF16)
    dq = dot_nn(ds, k)
    dk = dot_tn(ds, q)
    dv = dot_tn(probs, g)
    return out.astype(F32), dq, dk, dv


def lanes_of(head):
    return pl.ds(pl.multiple_of(head * HDIM, HDIM), HDIM)


def flat(ref, f, lanes):
    return ref[f, :, :, lanes].reshape(PLACES, HDIM).astype(F32)


def put_flat(ref, f, lanes, value):
    ref[f, :, :, lanes] = value.astype(BF16).reshape(COLS, 2, HDIM)


def norm_scales(refs, flat_x, scale):
    @pl.loop(0, 4)
    def _(f):
        for a, ref in enumerate(refs):
            total = jnp.zeros((PLACES, HDIM), F32)
            for h in range(HEADS):
                x = flat(ref, f, pl.ds(h * HDIM, HDIM))
                flat_x[a, f, h] = x
                total = total + x * x
            mean = jnp.sum(total, axis=-1, keepdims=True) * (1.0 / FEATURES)
            scale[a, f] = jnp.broadcast_to(lax.rsqrt(mean + EPSILON), (PLACES, HDIM))


def cut_block(arrays, g, fh, flat_x, refs, gain_ref, scale, rows, sent):
    for a in arrays:
        for f in range(2):
            for h in range(CHUNK):
                head = g * CHUNK + h
                if a < 2:
                    x = flat_x[a, 2 * fh + f, head] * scale[a, 2 * fh + f]
                    x = x * gain_ref[a:a + 1, lanes_of(head)]
                else:
                    x = flat(refs[a - 2], 2 * fh + f, lanes_of(head))
                rows[(a * 2 + f) * CHUNK + h, :PLACES, :] = x
        for row in range(2):
            for ch in range(2):
                start = row + 2 * HALF * ch
                main = []
                rest = []
                for h in range(CHUNK):
                    for f in range(2):
                        i = (a * 2 + f) * CHUNK + h
                        main.append(rows[i, pl.ds(start, 8, stride=2), :])
                        rest.append(rows[i, pl.ds(start + 16, 2, stride=2), :])
                block = jnp.concatenate(main + rest, axis=0).astype(BF16)
                sent[fh * 4 + row * 2 + ch, g, a * PART:(a + 1) * PART, :] = block


def join_block(g, fh, ret, out_ref, dv_ref, flat_x, flat_a, gain_ref, rows, scale, dots):
    for a in range(4):
        for row in range(2):
            for ch in range(2):
                start = row + 2 * HALF * ch
                block = ret[fh * 4 + row * 2 + ch, g, a * PART:(a + 1) * PART, :].astype(F32)
                for h in range(CHUNK):
                    for f in range(2):
                        i = (a * 2 + f) * CHUNK + h
                        main = h * MAIN + f * 8
                        rest = CHUNK * MAIN + h * REST + f * 2
                        rows[i, pl.ds(start, 8, stride=2), :] = block[main:main + 8]
                        rows[i, pl.ds(start + 16, 2, stride=2), :] = block[rest:rest + 2]
        for f in range(2):
            frame = 2 * fh + f
            total = dots[a - 1, frame] if a in (1, 2) else None
            for h in range(CHUNK):
                head = g * CHUNK + h
                value = rows[(a * 2 + f) * CHUNK + h, :PLACES, :]
                if a in (1, 2):
                    scaled = value * gain_ref[a - 1:a, lanes_of(head)]
                    flat_a[a - 1, frame, head] = scaled
                    total = total + scaled * flat_x[a - 1, frame, head]
                else:
                    put_flat((out_ref, dv_ref)[a // 3], frame, lanes_of(head), value)
            if a in (1, 2):
                dots[a - 1, frame] = total


def window_mask(where, bias):
    owner = lax.broadcasted_iota(jnp.int32, (TOKENS, TOKENS), 0)
    other = lax.broadcasted_iota(jnp.int32, (TOKENS, TOKENS), 1)
    octants = [jnp.where(i < 8 * MAIN, i >> 4, (i - 8 * MAIN) >> 2) for i in (owner, other)]
    t, r, c = where
    edge = (
        jnp.where(t == TIMES - 1, 4, 0)
        + jnp.where(r == GRID_ROWS - 1, 2, 0)
        + jnp.where(c == GRID_COLS - 1, 1, 0)
    )
    bias[...] = jnp.where(((octants[0] ^ octants[1]) & edge) == 0, 0.0, -1e30)


def attend(g, recv, res, bias, stage, sums):
    ends = [
        [
            recv[bits, g, a * PART + CHUNK * MAIN:(a + 1) * PART, :].astype(F32)
            for bits in range(8)
        ]
        for a in range(4)
    ]
    for h in range(CHUNK):
        window = []
        for a in range(4):
            start = a * PART + h * MAIN
            mains = [recv[bits, g, start:start + MAIN, :] for bits in range(8)]
            rests = [ends[a][bits][h * REST:(h + 1) * REST] for bits in range(8)]
            window.append(jnp.concatenate(mains + [jnp.concatenate(rests, axis=0).astype(BF16)], axis=0))
        results = head_attention(*window, bias[...])
        for a in range(4):
            start = a * PART + h * MAIN
            for bits in range(8):
                res[bits, g, start:start + MAIN, :] = results[a][bits * MAIN:(bits + 1) * MAIN].astype(BF16)
                rest = 8 * MAIN + bits * REST
                stage[a, bits, h * REST:(h + 1) * REST, :] = results[a][rest:rest + REST]
        for a in range(2):
            terms = results[1 + a].astype(BF16).astype(F32) * window[a].astype(F32)
            sums[g * CHUNK + h, a:a + 1, :] = jnp.sum(terms, axis=0, keepdims=True)
    for bits in range(8):
        for a in range(4):
            res[bits, g, a * PART + CHUNK * MAIN:(a + 1) * PART, :] = stage[a, bits].astype(BF16)


def window_kernel(
    q_hbm, k_hbm, v_hbm, g_hbm, gain_hbm,
    out_ref, dv_ref, flat_x, flat_a, scale, dots, gains_out_ref,
    q_ref, k_ref, v_ref, g_ref, gain_ref,
    rows, sent, recv, res, ret, bias, stage, sums, partial, slots,
    fsend, frecv, bsend, brecv, own_sem, gsend, grecv, in_sem,
):
    where = (
        lax.axis_index("tm"),
        lax.axis_index("space") // GRID_COLS,
        lax.axis_index("space") % GRID_COLS,
    )
    early = pl.ds(0, WIDTH)
    late = pl.ds(WIDTH, FEATURES - WIDTH)
    loads = [
        pltpu.make_async_copy(v_hbm.at[:, :, :, early], v_ref.at[:, :, :, early], in_sem.at[0]),
        pltpu.make_async_copy(g_hbm.at[:, :, :, early], g_ref.at[:, :, :, early], in_sem.at[1]),
        pltpu.make_async_copy(q_hbm, q_ref, in_sem.at[2]),
        pltpu.make_async_copy(k_hbm, k_ref, in_sem.at[3]),
        pltpu.make_async_copy(gain_hbm, gain_ref, in_sem.at[4]),
        pltpu.make_async_copy(v_hbm.at[:, :, :, late], v_ref.at[:, :, :, late], in_sem.at[5]),
        pltpu.make_async_copy(g_hbm.at[:, :, :, late], g_ref.at[:, :, :, late], in_sem.at[6]),
    ]
    for load in loads:
        load.start()

    rounds = gain_peers(where)
    barrier = pltpu.get_barrier_semaphore()
    for bits in range(1, 8):
        for sign in (-1, 1):
            pl.semaphore_signal(barrier, inc=1, device_id=shifted(where, bits, sign), device_id_type=MESH)
    for group in rounds:
        for device in group:
            pl.semaphore_signal(barrier, inc=1, device_id=device, device_id_type=MESH)

    def own_copy(g):
        return pltpu.make_async_copy(sent.at[7, g], recv.at[0, g], own_sem.at[0, g])

    def own_back(g):
        return pltpu.make_async_copy(res.at[0, g], ret.at[7, g], own_sem.at[1, g])

    def forth(g, bits):
        return pltpu.make_async_remote_copy(
            src_ref=sent.at[7 - bits, g],
            dst_ref=recv.at[bits, g],
            send_sem=fsend.at[g, bits],
            recv_sem=frecv.at[g, bits],
            device_id=shifted(where, bits, -1),
            device_id_type=MESH,
        )

    def forth_half(half, bits):
        part = pl.ds(half * 2 * PART, 2 * PART)
        sem = (CHUNKS, 0)[half]
        return pltpu.make_async_remote_copy(
            src_ref=sent.at[7 - bits, 0, part],
            dst_ref=recv.at[bits, 0, part],
            send_sem=fsend.at[sem, bits],
            recv_sem=frecv.at[sem, bits],
            device_id=shifted(where, bits, -1),
            device_id_type=MESH,
        )

    def back(g, bits):
        return pltpu.make_async_remote_copy(
            src_ref=res.at[bits, g],
            dst_ref=ret.at[7 - bits, g],
            send_sem=bsend.at[g, bits],
            recv_sem=brecv.at[g, bits],
            device_id=shifted(where, bits, 1),
            device_id_type=MESH,
        )

    def gain_copies(step):
        base = (0, 31)[step]
        copies = []
        for i, device in enumerate(rounds[step]):
            if step == 0:
                source = sums.at[pl.ds(first_row(device[1] // 8), 3)]
            else:
                source = partial.at[step - 1]
            copies.append(
                pltpu.make_async_remote_copy(
                    src_ref=source,
                    dst_ref=slots.at[base + i],
                    send_sem=gsend.at[base + i],
                    recv_sem=grecv.at[base + i],
                    device_id=device,
                    device_id_type=MESH,
                )
            )
        return copies

    def gain_start(step):
        for copy in gain_copies(step):
            copy.start()

    def gain_finish(step):
        base = (0, 31)[step]
        if step == 0:
            total = sums[pl.ds(first_row(lax.axis_index("space") // 8), 3)]
        else:
            total = partial[step - 1]
        for i, copy in enumerate(gain_copies(step)):
            copy.wait()
            total = total + slots[base + i]
        partial[step] = total

    def cut(arrays, g):
        @pl.loop(0, 2)
        def _(fh):
            cut_block(arrays, g, fh, flat_x, (v_ref, g_ref), gain_ref, scale, rows, sent)

    loads[0].wait()
    loads[1].wait()
    cut((2, 3), 0)
    pl.semaphore_wait(barrier, 14 + 31 + 7)
    for bits in FAR_FIRST:
        forth_half(1, bits).start()
    for load in loads[2:5]:
        load.wait()
    norm_scales((q_ref, k_ref), flat_x, scale)
    cut((0, 1), 0)
    for bits in FAR_FIRST:
        forth_half(0, bits).start()
    own_copy(0).start()
    for load in loads[5:]:
        load.wait()

    @pl.loop(1, CHUNKS)
    def _(g):
        cut((0, 1, 2, 3), g)
        for bits in FAR_FIRST:
            forth(g, bits).start()
        own_copy(g).start()

    window_mask(where, bias)

    @pl.loop(0, CHUNKS)
    def _(g):
        own_copy(g).wait()

        @pl.when(g == 0)
        def _():
            for bits in range(1, 8):
                forth_half(0, bits).wait_recv()
                forth_half(1, bits).wait_recv()

        @pl.when(g > 0)
        def _():
            for bits in range(1, 8):
                forth(g, bits).wait_recv()

        attend(g, recv, res, bias, stage, sums)

        @pl.when(g == CHUNKS - 1)
        def _():
            gain_start(0)

        for bits in FAR_FIRST:
            back(g, bits).start()
        own_back(g).start()

    dots[...] = jnp.zeros_like(dots)

    @pl.loop(0, CHUNKS)
    def _(g):
        @pl.when(g == 1)
        def _():
            gain_finish(0)
            gain_start(1)

        @pl.when(g == CHUNKS - 1)
        def _():
            gain_finish(1)
            width = FEATURES // 64
            first = lax.axis_index("space") * width
            row = first_row(lax.axis_index("space") // 8)
            line = first // HDIM - row
            lane = first % HDIM
            back_by = (HDIM - lane) % HDIM
            place = lax.broadcasted_iota(jnp.int32, (1, HDIM), 1)
            for a in range(2):
                parts = []
                for i in (line, (line + 1) % 3):
                    mean = partial[1, i, a:a + 1, :] / gain_ref[a:a + 1, lanes_of(row + i)]
                    parts.append(pltpu.roll(mean, back_by, 1))
                joined = jnp.where(place < HDIM - lane, parts[0], parts[1])
                gains_out_ref[a:a + 1, :] = joined[:, :width]
            for bits in range(1, 8):
                forth_half(0, bits).wait_send()
                forth_half(1, bits).wait_send()

            @pl.loop(1, CHUNKS)
            def _(i):
                for bits in range(1, 8):
                    forth(i, bits).wait_send()

            @pl.loop(0, CHUNKS - 1)
            def _(i):
                for bits in range(1, 8):
                    back(i, bits).wait_send()

        own_back(g).wait()
        for bits in range(1, 8):
            back(g, bits).wait_recv()

        @pl.loop(0, 2)
        def _(fh):
            join_block(g, fh, ret, out_ref, dv_ref, flat_x, flat_a, gain_ref, rows, scale, dots)

    for bits in range(1, 8):
        back(CHUNKS - 1, bits).wait_send()


def finish_kernel(
    out_vmem, dv_vmem, flat_x, flat_a, scale, dots, gains_vmem,
    out_ref, dq_ref, dk_ref, dv_ref, gains_ref, done, sem,
):
    whole = [
        pltpu.make_async_copy(out_vmem, out_ref, sem.at[0]),
        pltpu.make_async_copy(dv_vmem, dv_ref, sem.at[1]),
        pltpu.make_async_copy(gains_vmem, gains_ref, sem.at[2]),
    ]
    for copy in whole:
        copy.start()

    def frame(a, f):
        return pltpu.make_async_copy(done.at[a, f], (dq_ref, dk_ref)[a].at[f], sem.at[3 + 4 * a + f])

    @pl.loop(0, 4)
    def _(f):
        for a in range(2):
            r = scale[a, f]
            mean = jnp.sum(dots[a, f], axis=-1, keepdims=True) * (1.0 / FEATURES)
            factor = r * r * r * mean
            for h in range(HEADS):
                value = r * flat_a[a, f, h] - flat_x[a, f, h] * factor
                put_flat(done.at[a], f, pl.ds(h * HDIM, HDIM), value)
            frame(a, f).start()

    for copy in whole:
        copy.wait()
    for a in range(2):
        for f in range(4):
            frame(a, f).wait()


def windows(query, key, value, grad, gains):
    block = (8, CHUNKS, BLOCK, HDIM)
    natural = jax.ShapeDtypeStruct(query.shape, BF16)
    flat_rows = jax.ShapeDtypeStruct((2, 4, HEADS, PLACES, HDIM), F32)
    per_token = jax.ShapeDtypeStruct((2, 4, PLACES, HDIM), F32)
    slice_of_gains = jax.ShapeDtypeStruct((2, FEATURES // 64), F32)
    vmem = pl.BlockSpec(memory_space=pltpu.VMEM)
    hbm = pl.BlockSpec(memory_space=pltpu.HBM)
    query, key, value, grad, gains = [
        pltpu.with_memory_space_constraint(x, pltpu.HBM) for x in (query, key, value, grad, gains)
    ]
    held = pl.pallas_call(
        window_kernel,
        out_shape=(natural, natural, flat_rows, flat_rows, per_token, per_token, slice_of_gains),
        in_specs=[hbm] * 5,
        out_specs=(vmem,) * 7,
        scratch_shapes=[
            pltpu.VMEM(query.shape, BF16),
            pltpu.VMEM(query.shape, BF16),
            pltpu.VMEM(query.shape, BF16),
            pltpu.VMEM(query.shape, BF16),
            pltpu.VMEM((2, FEATURES), F32),
            pltpu.VMEM((8 * CHUNK, PLACES + 8, HDIM), F32),
            pltpu.VMEM(block, BF16),
            pltpu.VMEM(block, BF16),
            pltpu.VMEM(block, BF16),
            pltpu.VMEM(block, BF16),
            pltpu.VMEM((TOKENS, TOKENS), F32),
            pltpu.VMEM((4, 8, CHUNK * REST, HDIM), F32),
            pltpu.VMEM((HEADS, 2, HDIM), F32),
            pltpu.VMEM((2, 3, 2, HDIM), F32),
            pltpu.VMEM((38, 3, 2, HDIM), F32),
            pltpu.SemaphoreType.DMA((CHUNKS + 1, 8)),
            pltpu.SemaphoreType.DMA((CHUNKS + 1, 8)),
            pltpu.SemaphoreType.DMA((CHUNKS, 8)),
            pltpu.SemaphoreType.DMA((CHUNKS, 8)),
            pltpu.SemaphoreType.DMA((2, CHUNKS)),
            pltpu.SemaphoreType.DMA((38,)),
            pltpu.SemaphoreType.DMA((38,)),
            pltpu.SemaphoreType.DMA((7,)),
        ],
        compiler_params=pltpu.CompilerParams(
            collective_id=0, has_side_effects=True, vmem_limit_bytes=32 * 1024 * 1024
        ),
        name="windows",
    )(query, key, value, grad, gains)
    return pl.pallas_call(
        finish_kernel,
        out_shape=(natural,) * 4 + (slice_of_gains,),
        in_specs=[vmem] * 7,
        out_specs=(hbm,) * 5,
        scratch_shapes=[
            pltpu.VMEM((2,) + query.shape, BF16),
            pltpu.SemaphoreType.DMA((11,)),
        ],
        compiler_params=pltpu.CompilerParams(vmem_limit_bytes=32 * 1024 * 1024),
        name="finish",
    )(*held)


def per_device(query_in, key_in, value_in, out_grad, norm_gains):
    tokens = [x[:, 0].transpose(0, 2, 1, 3) for x in (query_in, key_in, value_in, out_grad)]
    outs = windows(*tokens, norm_gains)
    return tuple(out.transpose(0, 2, 1, 3)[:, None] for out in outs[:4]) + (outs[4],)


def solution(mesh):
    token = P("tm", "space", None, None, None)
    return jax.shard_map(
        per_device,
        mesh=mesh,
        in_specs=(token, token, token, token, P()),
        out_specs=(token, token, token, token, P(None, "space")),
        check_vma=False,
    )
```
